512 devices in a mesh: pipe: 16 (over z_lo, x), expert: 32 (over z_hi, y, core).
Axes of the slice: x: 4, y: 8, z: 8 (z_hi: 2, z_lo: 4; z = z_hi * 4 + z_lo), core: 2. Of those that a mesh axis runs over, the one named last changes fastest.
Arguments:
- stream_a: bfloat16 [16, 256, 3584], P('pipe', 'expert'), may hold values from -6 to 6
- stream_b: bfloat16 [16, 256, 3584], P('pipe', 'expert'), may hold values from -6 to 6
- routes: int32 [2, 2, 16, 256, 2], P(None, None, 'pipe', 'expert'), may hold values from 0 to 3, all different within a row; in each aligned block of 8 rows (0 to 7, 8 to 15, ..., all dimensions but the last counted through in order) at most 4 rows name the same one
- up_weight: bfloat16 [2, 16, 3584, 4096], P(None, 'pipe', None, 'expert'), as said below
- down_weight: bfloat16 [2, 16, 4096, 3584], P(None, 'pipe', 'expert'), as said below
- router_weight: bfloat16 [2, 16, 3584, 4], P(None, 'pipe'), as said below
Outputs:
- final_a: bfloat16 [16, 256, 3584], P('pipe', 'expert')
- final_b: bfloat16 [16, 256, 3584], P('pipe', 'expert')
- expert_load: float32 [16, 4], replicated
The draws below stay inside these ranges and needn't reach their ends.
Inputs may be any that keep to these rules, and one draw needn't show every extreme that they name: `routes`: in each device's 8 rows of one tick, stream and section, every expert is named by exactly 4 rows, and each row names 2 different experts. up_weight[1, i] equals up_weight[0, 15 - i]. down_weight[1, i] equals down_weight[0, 15 - i]. router_weight[1, i] equals router_weight[0, 15 - i].
All inputs are finite; a program needn't handle non-finite values.
Results may differ from the reference program's by a relative error of at most 0.0065.
Values may be sent and summed in bfloat16 or wider, within the bound.
A program may use at most 64 MiB of HBM per device.

```python
import math
import jax
import jax.numpy as jnp
import numpy as np
from jax import lax

D = 3584
H_EXP = 1024
EXPERTS = 4
TOP = 2
ROWS = 8
TICKS = 2
LAYERS = 16
TOK_SECTION = 256
CAP = 4
N_EXPERT = 32


def mirrored(layer_draw):
    return jnp.stack([layer_draw, layer_draw[::-1]]).astype(jnp.bfloat16)


def draw_up_weight(key, part):
    key = jax.random.fold_in(key, 11)
    layer_draw = jax.random.normal(key, (LAYERS, D, EXPERTS * H_EXP), jnp.float32) * D ** (-0.5)
    return mirrored(layer_draw)


def draw_down_weight(key, part):
    key = jax.random.fold_in(key, 23)
    layer_draw = jax.random.normal(key, (LAYERS, EXPERTS * H_EXP, D), jnp.float32) * H_EXP ** (-0.5)
    return mirrored(layer_draw)


def draw_router_weight(key, part):
    key = jax.random.fold_in(key, 37)
    layer_draw = jax.random.normal(key, (LAYERS, D, EXPERTS), jnp.float32) * (2.0 * D ** (-0.5))
    return mirrored(layer_draw)


def shard_levels(rng, extent, cuts, smallest, largest):
    loudness, own = 1.0, jax.random.fold_in(rng, 6)
    for axis_at, parts in cuts:
        draws = jnp.exp(jax.random.uniform(jax.random.fold_in(own, axis_at), (parts,), jnp.float32, smallest / len(cuts), largest / len(cuts)))
        loudness = loudness * jnp.repeat(draws, extent[axis_at] // parts).reshape([-1 if axis == axis_at else 1 for axis in range(len(extent))])
    return loudness


def assign_block(key, own, number, rows, amount, top, reach, lean):
    ranking = jax.random.permutation(key, amount)
    heavy_load, ordinary = load_shares(amount, rows * top, reach, lean, True), load_shares(amount, rows * top, reach, lean, False)
    places = jnp.arange(amount)

    def named(sizes, rotation):
        used = int((sizes > 0).sum())
        fixed = max(1, used // 4)
        passed = fixed + (places - fixed + rotation * (used - fixed)) % max(1, amount - fixed)
        return jnp.zeros((amount,), jnp.int32).at[ranking[jnp.where(places < fixed, places, passed)]].set(jnp.asarray(sizes, jnp.int32))

    sizes = jnp.where(number % 4 == 0, named(heavy_load, number // 4), named(ordinary, number - number // 4 - 1))
    mixed = jax.random.permutation(jax.random.fold_in(own, 3), amount)
    giver, sink = mixed[0:amount // 2 * 2:2], mixed[1:amount // 2 * 2:2]
    room = jnp.minimum(sizes[giver] - 1, reach - sizes[sink]) // 2
    room = jnp.where((giver == ranking[0]) | (sink == ranking[0]) | (sizes[sink] == 0), 0, jnp.maximum(room, 0))
    passed = jax.random.randint(jax.random.fold_in(own, 4), (amount // 2,), 0, 1 << 20) % (room + 1)
    sizes = sizes.at[giver].add(-passed).at[sink].add(passed)
    labels = jnp.searchsorted(jnp.cumsum(sizes), jnp.arange(rows * top), side="right").astype(jnp.int32)
    table = labels.reshape(top, rows).T
    table = table[jax.random.permutation(jax.random.fold_in(own, 1), rows)]
    rotation = jax.random.randint(jax.random.fold_in(own, 2), (rows, 1), 0, top)
    return jnp.take_along_axis(table, (jnp.arange(top)[None, :] + rotation) % top, axis=1)


def load_shares(count, total, limit, skew, full):
    portions = [(1 << 20) // math.isqrt(grade ** skew) + 1 for grade in range(1, count + 1)]
    largest = limit if full else min(limit, max(-(-total // count), total * portions[0] // sum(portions)))
    least = 1 if total - largest >= count - 1 else 0
    holding, rest = [largest] + [least] * (count - 1), total - largest - least * (count - 1)
    while rest > 0:
        free = [i for i in range(1, count) if holding[i] < largest] or [i for i in range(1, count) if holding[i] < limit]
        whole, budget = sum([portions[i] for i in free]), rest
        for i in free:
            more = min(limit - holding[i], max(1, budget * portions[i] // whole), rest)
            holding[i] = holding[i] + more
            rest = rest - more
    return np.array(holding)


def bell_draw(stream_key, shape, width, reach, cuts=(), kind=jnp.bfloat16):
    array = width * jax.random.normal(stream_key, shape, jnp.float32)
    if cuts:
        array = array * shard_levels(stream_key, shape, cuts, -0.22, 0.18)
    return jnp.clip(array, -reach, reach).astype(kind)


def setup_inputs(seed: int = 0) -> dict:
    streams_of = jax.random.split(jax.random.key(seed), 7)
    stream_a = bell_draw(streams_of[0], (LAYERS, TOK_SECTION, D), 1.0, 6.0, ((0, 16), (1, 32)))
    stream_b = bell_draw(streams_of[1], (LAYERS, TOK_SECTION, D), 1.0, 6.0, ((0, 16), (1, 32)))
    routes_keys = jax.random.split(jax.random.fold_in(streams_of[2], 1), TICKS * 2 * LAYERS * TOK_SECTION // ROWS)
    routes_turns = jax.random.permutation(jax.random.fold_in(streams_of[2], 3), TICKS * 2 * LAYERS * TOK_SECTION // ROWS)
    routes = jax.vmap(lambda own, number: assign_block(jax.random.fold_in(streams_of[2], 2), own, number, ROWS, EXPERTS, TOP, CAP, 0))(routes_keys, routes_turns).reshape((TICKS, 2, LAYERS, TOK_SECTION, TOP))
    up_weight = draw_up_weight(jax.random.fold_in(streams_of[6], 71), 0)
    down_weight = draw_down_weight(jax.random.fold_in(streams_of[6], 71), 0)
    router_weight = draw_router_weight(jax.random.fold_in(streams_of[6], 71), 0)
    return dict(stream_a=stream_a, stream_b=stream_b, routes=routes, up_weight=up_weight, down_weight=down_weight, router_weight=router_weight)


EPS = 1e-06

def normalize(section_rows):
    widened = section_rows.astype(jnp.float32)
    return (widened * lax.rsqrt(lax.optimization_barrier(jnp.mean(widened * widened, axis=-1, keepdims=True)) + EPS)).astype(jnp.bfloat16)

def routing(normed, router, picked):
    experts = router.shape[-1]
    affinity = jax.nn.sigmoid(jnp.dot(normed, router, preferred_element_type=jnp.float32))
    member = (picked[:, :, None] == jnp.arange(experts, dtype=jnp.int32)[None, None, :]).astype(jnp.float32)
    chosen = lax.optimization_barrier(jnp.sum(member * affinity[:, None, :], axis=2))
    shares = chosen / lax.optimization_barrier(jnp.sum(chosen, axis=1, keepdims=True))
    weights = lax.optimization_barrier(jnp.sum(shares[:, :, None] * member, axis=1))
    selected = lax.optimization_barrier(jnp.sum(member, axis=1))
    return (weights, selected)

def apply_section(section_rows, lift_weight, lower_weight, router, picked):
    normed = normalize(section_rows)
    weights, selected = routing(normed, router, picked)
    experts = router.shape[-1]
    token_count = section_rows.shape[0]
    capacity = token_count * picked.shape[1] // experts
    group_size = N_EXPERT // experts
    hidden_width = lift_weight.shape[1] // experts
    slice_width = hidden_width // group_size
    features = section_rows.shape[1]
    total = jnp.zeros((token_count, features), jnp.float32)
    for expert in range(experts):
        flags = selected[:, expert].astype(jnp.int32)
        chosen_rows = jnp.argsort(1 - flags, stable=True)[:capacity].astype(jnp.int32)
        gathered = normed[chosen_rows]
        hidden = jax.nn.silu(jnp.dot(gathered, lift_weight[:, expert * hidden_width:(expert + 1) * hidden_width], preferred_element_type=jnp.float32)).astype(jnp.bfloat16)
        lower_part = lower_weight[expert * hidden_width:(expert + 1) * hidden_width].reshape(group_size, slice_width, features)
        pieces = jnp.einsum('rgk,gkd->grd', hidden.reshape(capacity, group_size, slice_width).astype(jnp.float32), lower_part.astype(jnp.float32), precision=lax.Precision.HIGHEST)
        rounded = lax.optimization_barrier(pieces.astype(jnp.bfloat16)).astype(jnp.float32)
        result = lax.optimization_barrier(jnp.sum(rounded, axis=0))
        total = total.at[chosen_rows].add(weights[chosen_rows, expert][:, None] * result)
    return ((section_rows.astype(jnp.float32) + total).astype(jnp.bfloat16), lax.optimization_barrier(jnp.sum(weights, axis=0)))

def apply_layer(bundle):
    return apply_section(bundle[0], bundle[1], bundle[2], bundle[3], bundle[4])

def reference(stream_a, stream_b, routes, up_weight, down_weight, router_weight):
    current = [stream_a, stream_b]
    load_sum = jnp.zeros((LAYERS, EXPERTS), jnp.float32)
    for step_index in range(TICKS):
        if step_index > 0:
            current = [jnp.roll(current[0], 1, axis=0), jnp.roll(current[1], -1, axis=0)]
        updated = []
        for stream in range(2):
            outcome, masses = lax.map(apply_layer, (current[stream], up_weight[stream], down_weight[stream], router_weight[stream], routes[step_index, stream]))
            updated.append(outcome)
            if stream == 0:
                load_sum = load_sum + masses
            else:
                load_sum = load_sum + masses[::-1]
        current = updated
    return (current[0], current[1], load_sum / (2 * TICKS * TOK_SECTION))
```

```python
import jax
import jax.numpy as jnp
from jax import lax
from jax.experimental import pallas as pl
from jax.experimental.pallas import tpu as pltpu
from jax.sharding import PartitionSpec as P

TICKS = 2
EPS = 1e-06
QUARTERS = 4
CAP = 4
SIDE = 8
MESH = pl.DeviceIdType.MESH

Z_OUT, Y_OWN, Y_PEER, Y_BACK, Z_BACK, RELAY = range(6)
BLOCK = 16


def kernel(
    sa, sb, routes, router, up, down,
    out_a, out_b, out_load,
    u, w, tx, zrx, rx, back, crx, ztx, zc, xtx, xr, mtx, mrx,
    send, recv, wlocal, wsend, wrecv, msend, mrecv,
):
    quarter = u.shape[1]
    features = QUARTERS * quarter
    pipe = lax.axis_index("pipe")
    ex = lax.axis_index("expert")
    zh = ex // 16
    y = (ex // 2) % SIDE
    core = ex % 2
    sibling = {"expert": ex + 1 - 2 * core}
    zpeer = {"expert": (1 - zh) * 16 + y * 2 + core}

    def chip_y(to):
        return {"expert": zh * 16 + to * 2 + core}

    def step_y(i):
        return lax.rem(y + jnp.where(i % 2 == 0, i // 2 + 1, SIDE - 1 - i // 2), SIDE)

    px, pz = pipe % 4, pipe // 4
    x_mates = [{"pipe": pz * 4 + (px + k) % 4} for k in range(1, 4)]
    z_mates = [{"pipe": ((pz + k) % 4) * 4 + px} for k in range(1, 4)]
    ahead = {"pipe": (pipe + 1) % 16}
    behind = {"pipe": (pipe + 15) % 16}

    def weight_parts(s, which):
        if which == 0:
            return [
                (
                    up.at[s, 0, pl.ds(q * quarter, quarter), :],
                    u.at[s, :, pl.ds(pl.multiple_of(q * 256 + core * 128, 128), 128)],
                )
                for q in range(QUARTERS)
            ]
        return [(down.at[s, 0], w.at[s, pl.ds(pl.multiple_of(core * 128, 128), 128), :])]

    for s in range(2):
        for which in range(2):
            for src, dst in weight_parts(s, which):
                pltpu.make_async_copy(src, dst, wlocal.at[s, which]).start()

    barrier = pltpu.get_barrier_semaphore()

    def greet(device):
        pl.semaphore_signal(barrier, inc=1, device_id=device, device_id_type=MESH)

    for device in [sibling, zpeer, ahead, behind] + x_mates + z_mates:
        greet(device)

    @pl.loop(0, SIDE - 1)
    def _(i):
        greet(chip_y(step_y(i)))

    pl.semaphore_wait(barrier, 4 + 6 + SIDE - 1)

    def remote(src, dst, t, s, kind, device):
        return pltpu.make_async_remote_copy(
            src_ref=src, dst_ref=dst, send_sem=send.at[t, s, kind],
            recv_sem=recv.at[t, s, kind], device_id=device, device_id_type=MESH,
        )

    def drain(ref, sem):
        pltpu.make_async_copy(ref, ref, sem).wait()

    def half_of_weight(s, which):
        return u.at[s, :, pl.ds(0, 512)] if which == 0 else w.at[s, pl.ds(0, 128), :]

    def send_weights(s):
        for which in range(2):
            for src, dst in weight_parts(s, which):
                pltpu.make_async_remote_copy(
                    src_ref=src, dst_ref=dst, send_sem=wsend.at[s, which],
                    recv_sem=wrecv.at[s, which], device_id=sibling, device_id_type=MESH,
                ).start()

    lane4 = lax.broadcasted_iota(jnp.int32, (8, 4), 1)
    low8 = (
        lax.broadcasted_iota(jnp.int32, (8, 8), 0) > lax.broadcasted_iota(jnp.int32, (8, 8), 1)
    ).astype(jnp.bfloat16)
    row64 = lax.broadcasted_iota(jnp.int32, (64, 4), 0)
    expert_hot = (row64 // BLOCK == lax.broadcasted_iota(jnp.int32, (64, 4), 1)).astype(
        jnp.bfloat16
    )
    row_t = lax.broadcasted_iota(jnp.int32, (64, 32), 0)
    col_t = lax.broadcasted_iota(jnp.int32, (64, 32), 1)
    same_quarter = (row_t // 4) % 4 == col_t // 8
    slot_t = (row_t % 4).astype(jnp.float32)

    def pieces(t, s):
        if t == 0:
            ref = sa if s == 0 else sb
            return [
                ref[0, :, q * quarter : (q + 1) * quarter].astype(jnp.float32)
                for q in range(QUARTERS)
            ]
        rows = xr[s].astype(jnp.float32)
        return [rows[q * 8 : (q + 1) * 8] for q in range(QUARTERS)]

    def prepare(t, s):
        x = pieces(t, s)
        total = sum(jnp.sum(part * part, axis=1, keepdims=True) for part in x)
        scale = lax.rsqrt(total / features + EPS)
        normed = [part * scale for part in x]
        normed4 = jnp.concatenate(normed, axis=0).astype(jnp.bfloat16)
        logits = sum(
            jnp.dot(
                normed[q].astype(jnp.bfloat16),
                router[s, 0, q * quarter : (q + 1) * quarter, :],
                preferred_element_type=jnp.float32,
            )
            for q in range(QUARTERS)
        )
        affinity = jax.nn.sigmoid(logits)
        picked = routes[t, s, 0]
        member = [(picked[:, j : j + 1] == lane4).astype(jnp.float32) for j in range(2)]
        chosen = [jnp.sum(m * affinity, axis=1, keepdims=True) for m in member]
        both = chosen[0] + chosen[1]
        gates = (chosen[0] / both) * member[0] + (chosen[1] / both) * member[1]
        selected = member[0] + member[1]
        before = jnp.dot(low8, selected.astype(jnp.bfloat16), preferred_element_type=jnp.float32)
        slot = jnp.where(selected > 0, before, -1.0)
        slot4 = jnp.concatenate([slot] * QUARTERS, axis=0).astype(jnp.bfloat16)
        slot_of = lax.dot_general(
            expert_hot, slot4, (((1,), (1,)), ((), ())), preferred_element_type=jnp.float32
        )
        place = jnp.where(same_quarter & (slot_of == slot_t), 1.0, 0.0).astype(jnp.bfloat16)
        tx[t, s] = jnp.dot(place, normed4, preferred_element_type=jnp.float32).astype(jnp.bfloat16)
        return gates, slot

    def block(index):
        return pl.ds(pl.multiple_of(index * BLOCK, BLOCK), BLOCK)

    def dispatch(t, s):
        remote(
            tx.at[t, s, pl.ds(pl.multiple_of((1 - zh) * 32, 32), 32)], zrx.at[t, s],
            t, s, Z_OUT, zpeer,
        ).start()

        @pl.loop(0, SIDE - 1)
        def _(i):
            to = step_y(i)
            remote(
                tx.at[t, s, block(zh * 2 + to // 4)], rx.at[t, s, block(y * 2 + zh)],
                t, s, Y_OWN, chip_y(to),
            ).start()

        rx[t, s, block(y * 2 + zh)] = tx[t, s, block(zh * 2 + y // 4)]

    def dispatch_peer(t, s):
        drain(zrx.at[t, s], recv.at[t, s, Z_OUT])

        @pl.loop(0, SIDE - 1)
        def _(i):
            to = step_y(i)
            remote(
                zrx.at[t, s, block(to // 4)], rx.at[t, s, block(y * 2 + 1 - zh)],
                t, s, Y_PEER, chip_y(to),
            ).start()

        rx[t, s, block(y * 2 + 1 - zh)] = zrx[t, s, block(y // 4)]

    def experts(t, s):
        for kind in (Y_OWN, Y_PEER):
            drain(rx.at[t, s, pl.ds(0, (SIDE - 1) * BLOCK)], recv.at[t, s, kind])
        if t == 0:
            drain(u.at[s, :, pl.ds(0, 512)], wlocal.at[s, 0])
            drain(u.at[s, :, pl.ds(0, 512)], wrecv.at[s, 0])
        arrived = rx[t, s]
        lower = lax.broadcasted_iota(jnp.int32, (16, 8, 256), 1) < 4
        lifted = [
            jnp.dot(
                arrived, u[s, :, q * 256 : (q + 1) * 256], preferred_element_type=jnp.float32
            ).reshape(16, 2, 8, 256)
            for q in range(QUARTERS)
        ]
        part = jnp.where(lower, lifted[0][:, 0], lifted[1][:, 0]) + jnp.where(
            lower, lifted[2][:, 1], lifted[3][:, 1]
        )
        part = part.reshape(128, 256)
        lower2 = lax.broadcasted_iota(jnp.int32, (128, 256), 0) % 8 < 4
        other = jnp.where(lower2, pltpu.roll(part, 124, 0), pltpu.roll(part, 4, 0))
        hidden = jax.nn.silu(part + other).astype(jnp.bfloat16)
        if t == 0:
            drain(w.at[s, pl.ds(0, 128), :], wlocal.at[s, 1])
            drain(w.at[s, pl.ds(0, 128), :], wrecv.at[s, 1])
        lower3 = lax.broadcasted_iota(jnp.int32, (128, quarter), 0) % 8 < 4
        halves = []
        for h in range(2):
            two = [
                jnp.dot(
                    hidden, w[s, :, q * quarter : (q + 1) * quarter],
                    preferred_element_type=jnp.float32,
                )
                for q in (2 * h, 2 * h + 1)
            ]
            halves.append(jnp.where(lower3, two[0], two[1]).reshape(16, 1, 8, quarter))
        back[t, s] = (
            jnp.concatenate(halves, axis=1).reshape(256, quarter).astype(jnp.bfloat16)
        )

        def pair(index):
            return pl.ds(pl.multiple_of(index * 32, 32), 32)

        @pl.loop(0, SIDE - 1)
        def _(i):
            to = step_y(i)
            remote(
                back.at[t, s, pair(to)], crx.at[t, s, pair(y)], t, s, Y_BACK, chip_y(to)
            ).start()

        crx[t, s, pair(y)] = back[t, s, pair(y)]

    def sum_back(t, s):
        drain(crx.at[t, s, pl.ds(0, (SIDE - 1) * 32)], recv.at[t, s, Y_BACK])

        def over_line(zsrc, h):
            return sum(
                crx[t, s, block((h * 4 + k) * 2 + zsrc)].astype(jnp.float32) for k in range(4)
            )

        for h in range(2):
            ztx[t, s, h * BLOCK : (h + 1) * BLOCK] = over_line(1 - zh, h).astype(jnp.bfloat16)
        remote(ztx.at[t, s], zc.at[t, s], t, s, Z_BACK, zpeer).start()
        return [over_line(zh, h) for h in range(2)]

    def finish(t, s, own, gates, slot):
        drain(zc.at[t, s], recv.at[t, s, Z_BACK])
        other = [zc[t, s, h * BLOCK : (h + 1) * BLOCK].astype(jnp.float32) for h in range(2)]
        x = pieces(t, s)
        first = zh == 0
        terms = []
        for h in range(2):
            for sums, low in ((own[h], first), (other[h], jnp.logical_not(first))):
                gate = jnp.where(low, gates[:, h : h + 1], gates[:, 2 + h : 3 + h])
                place = jnp.where(low, slot[:, h : h + 1], slot[:, 2 + h : 3 + h])
                for c in range(CAP):
                    terms.append((sums, c, jnp.where(place == c, gate, 0.0)))
        rows = []
        for q in range(QUARTERS):
            total = x[q]
            for sums, c, factor in terms:
                total = total + factor * sums[q * 4 + c : q * 4 + c + 1, :]
            rows.append(total)
        if t + 1 < TICKS:
            xtx[s] = jnp.concatenate(rows, axis=0).astype(jnp.bfloat16)
            remote(xtx.at[s], xr.at[s], t, s, RELAY, ahead if s == 0 else behind).start()
        else:
            ref = out_a if s == 0 else out_b
            for q in range(QUARTERS):
                ref[0, :, q * quarter : (q + 1) * quarter] = rows[q].astype(jnp.bfloat16)

    y_mates = [chip_y(lax.rem(y + k, SIDE)) for k in range(1, SIDE)]
    rounds = [[sibling], y_mates, [zpeer], x_mates, z_mates]

    def mass_send(k):
        for i, device in enumerate(rounds[k]):
            pltpu.make_async_remote_copy(
                src_ref=mtx.at[k], dst_ref=mrx.at[k, i], send_sem=msend.at[k],
                recv_sem=mrecv.at[k], device_id=device, device_id_type=MESH,
            ).start()

    def mass_take(k):
        count = len(rounds[k])
        drain(mrx.at[k, pl.ds(0, count)], mrecv.at[k])
        return sum((mrx[k, i] for i in range(count)), mtx[k])

    def mass_step(k):
        mtx[k + 1] = mass_take(k)
        mass_send(k + 1)

    masses = [None, None]
    for t in range(TICKS):
        routed = [None, None]
        for s in range(2):
            if t > 0:
                drain(xr.at[s], recv.at[t - 1, s, RELAY])
            routed[s] = prepare(t, s)
            dispatch(t, s)
            mass = jnp.sum(routed[s][0], axis=0, keepdims=True)
            masses[s] = mass if t == 0 else masses[s] + mass
            if t == 0:
                send_weights(s)
        if t == TICKS - 1:
            row = lax.broadcasted_iota(jnp.int32, (16, 4), 0)
            table = jnp.where(row == pipe, masses[0], 0.0) + jnp.where(
                row == 15 - pipe, masses[1], 0.0
            )
            mtx[0] = jnp.zeros_like(mtx[0])
            mtx[0, :, 0:4] = table
            mass_send(0)
        last = t == TICKS - 1
        for s in range(2):
            dispatch_peer(t, s)
        for s in range(2):
            if last:
                mass_step(s)
            experts(t, s)
        own = []
        for s in range(2):
            if last:
                mass_step(2 + s)
            own.append(sum_back(t, s))
        for s in range(2):
            finish(t, s, own[s], *routed[s])
    out_load[...] = mass_take(4)[:, 0:4] / (2 * TICKS * 8 * 32)

    for s in range(2):
        for which in range(2):
            drain(half_of_weight(s, which), wsend.at[s, which])
    for k in range(5):
        drain(mrx.at[k, pl.ds(0, len(rounds[k]))], msend.at[k])
    for t in range(TICKS):
        for s in range(2):
            drain(zrx.at[t, s], send.at[t, s, Z_OUT])
            for kind in (Y_OWN, Y_PEER):
                drain(rx.at[t, s, pl.ds(0, (SIDE - 1) * BLOCK)], send.at[t, s, kind])
            drain(crx.at[t, s, pl.ds(0, (SIDE - 1) * 32)], send.at[t, s, Y_BACK])
            drain(zc.at[t, s], send.at[t, s, Z_BACK])
            if t + 1 < TICKS:
                drain(xr.at[s], send.at[t, s, RELAY])


def shards(stream_a, stream_b, routes, up_weight, down_weight, router_weight):
    features = stream_a.shape[2]
    quarter = features // QUARTERS
    vmem = pl.BlockSpec(memory_space=pltpu.VMEM)
    hbm = pl.BlockSpec(memory_space=pl.ANY)
    bf16, f32 = jnp.bfloat16, jnp.float32
    return pl.pallas_call(
        kernel,
        out_shape=(
            jax.ShapeDtypeStruct(stream_a.shape, bf16),
            jax.ShapeDtypeStruct(stream_b.shape, bf16),
            jax.ShapeDtypeStruct((16, 4), f32),
        ),
        in_specs=[vmem, vmem, vmem, vmem, hbm, hbm],
        out_specs=(vmem, vmem, vmem),
        scratch_shapes=[
            pltpu.VMEM((2, quarter, QUARTERS * 256), bf16),
            pltpu.VMEM((2, 256, features), bf16),
            pltpu.VMEM((TICKS, 2, 64, quarter), bf16),
            pltpu.VMEM((TICKS, 2, 32, quarter), bf16),
            pltpu.VMEM((TICKS, 2, 256, quarter), bf16),
            pltpu.VMEM((TICKS, 2, 256, quarter), bf16),
            pltpu.VMEM((TICKS, 2, 256, quarter), bf16),
            pltpu.VMEM((TICKS, 2, 32, quarter), bf16),
            pltpu.VMEM((TICKS, 2, 32, quarter), bf16),
            pltpu.VMEM((2, 32, quarter), bf16),
            pltpu.VMEM((2, 32, quarter), bf16),
            pltpu.VMEM((5, 16, 128), f32),
            pltpu.VMEM((5, SIDE - 1, 16, 128), f32),
            pltpu.SemaphoreType.DMA((TICKS, 2, 6)),
            pltpu.SemaphoreType.DMA((TICKS, 2, 6)),
            pltpu.SemaphoreType.DMA((2, 2)),
            pltpu.SemaphoreType.DMA((2, 2)),
            pltpu.SemaphoreType.DMA((2, 2)),
            pltpu.SemaphoreType.DMA((5,)),
            pltpu.SemaphoreType.DMA((5,)),
        ],
        compiler_params=pltpu.CompilerParams(
            collective_id=0, has_side_effects=True, vmem_limit_bytes=48 * 2**20
        ),
        name="relay",
    )(stream_a, stream_b, routes, router_weight, up_weight, down_weight)


def solution(mesh):
    return jax.shard_map(
        shards,
        mesh=mesh,
        in_specs=(
            P("pipe", "expert", None),
            P("pipe", "expert", None),
            P(None, None, "pipe", "expert", None),
            P(None, "pipe", None, "expert"),
            P(None, "pipe", "expert", None),
            P(None, "pipe", None, None),
        ),
        out_specs=(P("pipe", "expert", None), P("pipe", "expert", None), P()),
        check_vma=False,
    )
```

```python
import jax
import jax.numpy as jnp
from jax import lax
from jax.experimental import pallas as pl
from jax.experimental.pallas import tpu as pltpu
from jax.sharding import PartitionSpec as P

TICKS = 2
EPS = 1e-06
QUARTERS = 4
CAP = 4
SIDE = 8
SECTIONS = 16
BLOCK = 16
MESH = pl.DeviceIdType.MESH

TO_OWN, TO_OTHER, ON_OWN, ON_OTHER, SWAP_OWN, SWAP_OTHER, HOME, RELAY = range(8)
KINDS = 8


def kernel(
    sa, sb, routes, router, up, down,
    out_a, out_b, out_load,
    u, w, tx, rx, mine, swap_tx, swap_rx, home_tx, home_rx, xtx, xr,
    picks, picks_next, centroids, centroids_next, mtx, mrx,
    send, recv, wlocal, wsend, wrecv, psend, precv, msend, mrecv,
):
    quarter = u.shape[1]
    features = QUARTERS * quarter
    f32, bf16 = jnp.float32, jnp.bfloat16
    pipe = lax.axis_index("pipe")
    ex = lax.axis_index("expert")
    zh = ex // 16
    y = (ex // 2) % SIDE
    core = ex % 2
    turn = 1 - 2 * (y % 2)
    sibling = {"expert": ex + 1 - 2 * core}
    mate = {"expert": ex + 2 * turn}
    ahead = (pipe + 1) % SECTIONS
    behind = (pipe + SECTIONS - 1) % SECTIONS

    def at(plane, to):
        return plane * 16 + to * 2 + core

    targets = [(y + turn * step + SIDE) % SIDE for step in (0, -1, 2, -3)]
    sources = [(y - turn * k + SIDE) % SIDE for k in range(4)]

    px, pz = pipe % 4, pipe // 4
    x_mates = [{"pipe": pz * 4 + (px + k) % 4} for k in range(1, 4)]
    z_mates = [{"pipe": ((pz + k) % 4) * 4 + px} for k in range(1, 4)]
    y_mates = [{"expert": at(zh, (y + k) % SIDE)} for k in range(1, SIDE)]

    def weight_parts(s, which):
        if which == 0:
            return [
                (
                    up.at[s, 0, pl.ds(q * quarter, quarter), :],
                    u.at[s, :, pl.ds(pl.multiple_of(q * 256 + core * 128, 128), 128)],
                )
                for q in range(QUARTERS)
            ]
        return [(down.at[s, 0], w.at[s, pl.ds(pl.multiple_of(core * 128, 128), 128), :])]

    barrier = pltpu.get_barrier_semaphore()

    def greet(device):
        pl.semaphore_signal(barrier, inc=1, device_id=device, device_id_type=MESH)

    greeted = [sibling] + x_mates + z_mates + y_mates
    greeted += [{"expert": at(1 - zh, to)} for to in range(SIDE)]
    for section in (ahead, behind):
        for plane in (zh, 1 - zh):
            greeted += [{"pipe": section, "expert": at(plane, to)} for to in sources]
    for device in greeted:
        greet(device)

    for s in range(2):
        for which in range(2):
            for src, dst in weight_parts(s, which):
                pltpu.make_async_copy(src, dst, wlocal.at[s, which]).start()

    def remote(src, dst, t, s, kind, device):
        return pltpu.make_async_remote_copy(
            src_ref=src, dst_ref=dst, send_sem=send.at[t, s, kind],
            recv_sem=recv.at[t, s, kind], device_id=device, device_id_type=MESH,
        )

    def drain(ref, sem):
        pltpu.make_async_copy(ref, ref, sem).wait()

    def half_of_weight(s, which):
        return u.at[s, :, pl.ds(0, 512)] if which == 0 else w.at[s, pl.ds(0, 128), :]

    def send_weights(s):
        for which in range(2):
            for src, dst in weight_parts(s, which):
                pltpu.make_async_remote_copy(
                    src_ref=src, dst_ref=dst, send_sem=wsend.at[s, which],
                    recv_sem=wrecv.at[s, which], device_id=sibling, device_id_type=MESH,
                ).start()

    def iota(shape, dim):
        return lax.broadcasted_iota(jnp.int32, shape, dim)

    def across(a, b):
        return lax.dot_general(a, b, (((1,), (1,)), ((), ())), preferred_element_type=f32)

    lane4 = iota((8, 4), 1).astype(f32)
    low8 = (iota((8, 8), 0) > iota((8, 8), 1)).astype(bf16)
    eye8 = (iota((8, 8), 0) == iota((8, 8), 1)).astype(bf16)
    expert_hot = (iota((64, 4), 0) // BLOCK == iota((64, 4), 1)).astype(bf16)
    row_t, col_t = iota((64, 32), 0), iota((64, 32), 1)
    same_quarter = (row_t // 4) % 4 == col_t // 8
    slot_t = (row_t % 4).astype(f32)

    for s in range(2):
        for t in range(TICKS):
            picks[t, s, :, 0:2] = across(eye8, routes[t, s, 0].astype(f32).astype(bf16))
        centroids[s] = jnp.concatenate(
            [
                router[s, 0, :, q * quarter : (q + 1) * quarter].astype(f32)
                for q in range(QUARTERS)
            ],
            axis=0,
        ).astype(bf16)

    def send_ahead_of_relay():
        for s, section in ((0, behind), (1, ahead)):
            for i, (src, dst) in enumerate(
                ((picks.at[1, s], picks_next.at[s]), (centroids.at[s], centroids_next.at[s]))
            ):
                pltpu.make_async_remote_copy(
                    src_ref=src, dst_ref=dst, send_sem=psend.at[s, i], recv_sem=precv.at[s, i],
                    device_id={"pipe": section}, device_id_type=MESH,
                ).start()

    def first_rows(s):
        ref = sa if s == 0 else sb
        return [
            ref[0, :, q * quarter : (q + 1) * quarter].astype(f32) for q in range(QUARTERS)
        ]

    def relayed_rows(ref, s):
        rows = ref[s].astype(f32)
        return [rows[q * 8 : (q + 1) * 8] for q in range(QUARTERS)]

    def route(x, picked, central):
        total = sum(jnp.sum(part * part, axis=1, keepdims=True) for part in x)
        scale = lax.rsqrt(total / features + EPS)
        normed4 = jnp.concatenate([part * scale for part in x], axis=0).astype(bf16)
        mixed = across(normed4, central)
        logits = sum(
            mixed[q * 8 : (q + 1) * 8, q * 4 : (q + 1) * 4] for q in range(QUARTERS)
        )
        affinity = jax.nn.sigmoid(logits)
        member = [(picked[:, j : j + 1] == lane4).astype(f32) for j in range(2)]
        chosen = [jnp.sum(m * affinity, axis=1, keepdims=True) for m in member]
        both = chosen[0] + chosen[1]
        gates = (chosen[0] / both) * member[0] + (chosen[1] / both) * member[1]
        selected = member[0] + member[1]
        before = jnp.dot(low8, selected.astype(bf16), preferred_element_type=f32)
        slot = jnp.where(selected > 0, before, -1.0)
        return normed4, gates, slot

    def pack(t, s, normed4, slot):
        slot_of = across(expert_hot, jnp.concatenate([slot] * QUARTERS, axis=0).astype(bf16))
        place = jnp.where(same_quarter & (slot_of == slot_t), 1.0, 0.0).astype(bf16)
        tx[t, s] = jnp.dot(place, normed4, preferred_element_type=f32).astype(bf16)

    def block(index):
        if isinstance(index, int):
            return pl.ds(index * BLOCK, BLOCK)
        return pl.ds(pl.multiple_of(index * BLOCK, BLOCK), BLOCK)

    def blocks(first, count):
        return pl.ds(first * BLOCK, count * BLOCK)

    def dispatch(t, s):
        for plane, kind, base in ((1 - zh, TO_OTHER, 4), (zh, TO_OWN, 0)):
            for k, to in enumerate(targets):
                src = block(plane * 2 + to // 4)
                if t == 0 and base == 0 and k == 0:
                    rx[t, s, block(0)] = tx[t, s, src]
                    continue
                device = {"expert": at(plane, to)}
                if t > 0:
                    device["pipe"] = ahead if s == 0 else behind
                remote(
                    tx.at[t, s, src], rx.at[t, s, block(base + k)], t, s, kind, device
                ).start()

    def pass_on(t, s):
        own = blocks(1, 3) if t == 0 else blocks(0, 4)
        drain(rx.at[t, s, own], recv.at[t, s, TO_OWN])
        remote(rx.at[t, s, blocks(0, 4)], rx.at[t, s, blocks(8, 4)], t, s, ON_OWN, mate).start()
        drain(rx.at[t, s, blocks(4, 4)], recv.at[t, s, TO_OTHER])
        remote(rx.at[t, s, blocks(4, 4)], rx.at[t, s, blocks(12, 4)], t, s, ON_OTHER, mate).start()

    def experts(t, s):
        drain(rx.at[t, s, blocks(8, 4)], recv.at[t, s, ON_OWN])
        drain(rx.at[t, s, blocks(12, 4)], recv.at[t, s, ON_OTHER])
        if t == 0:
            drain(half_of_weight(s, 0), wlocal.at[s, 0])
            drain(half_of_weight(s, 0), wrecv.at[s, 0])
        arrived = rx[t, s]
        lower = iota((16, 8, 256), 1) < 4
        lifted = [
            jnp.dot(
                arrived, u[s, :, q * 256 : (q + 1) * 256], preferred_element_type=f32
            ).reshape(16, 2, 8, 256)
            for q in range(QUARTERS)
        ]
        part = jnp.where(lower, lifted[0][:, 0], lifted[1][:, 0]) + jnp.where(
            lower, lifted[2][:, 1], lifted[3][:, 1]
        )
        part = part.reshape(128, 256)
        lower2 = iota((128, 256), 0) % 8 < 4
        other = jnp.where(lower2, pltpu.roll(part, 124, 0), pltpu.roll(part, 4, 0))
        hidden = jax.nn.silu(part + other).astype(bf16)
        if t == 0:
            drain(half_of_weight(s, 1), wlocal.at[s, 1])
            drain(half_of_weight(s, 1), wrecv.at[s, 1])
        lower3 = iota((128, quarter), 0) % 8 < 4
        halves = []
        for h in range(2):
            two = [
                jnp.dot(
                    hidden, w[s, :, q * quarter : (q + 1) * quarter], preferred_element_type=f32
                )
                for q in (2 * h, 2 * h + 1)
            ]
            halves.append(jnp.where(lower3, two[0], two[1]).reshape(16, 1, 8, quarter))
        both = jnp.concatenate(halves, axis=1).reshape(256, quarter)
        mine[s] = both[0:128]
        swap_tx[t, s] = both[128:256].astype(bf16)
        for kind, first in ((SWAP_OTHER, 4), (SWAP_OWN, 0)):
            remote(
                swap_tx.at[t, s, blocks(first, 4)], swap_rx.at[t, s, blocks(first, 4)],
                t, s, kind, mate,
            ).start()

    def send_home(t, s):
        slot = zh * 4 + y // 2
        for plane, kind, base in ((1 - zh, SWAP_OTHER, 4), (zh, SWAP_OWN, 0)):
            rows = blocks(base, 4)
            drain(swap_rx.at[t, s, rows], recv.at[t, s, kind])
            home_tx[t, s, rows] = (mine[s, rows] + swap_rx[t, s, rows].astype(f32)).astype(bf16)
            for k, to in enumerate(sources):
                if base == 0 and k == 0:
                    home_rx[t, s, block(slot)] = home_tx[t, s, block(0)]
                    continue
                remote(
                    home_tx.at[t, s, block(base + k)], home_rx.at[t, s, block(slot)],
                    t, s, HOME, {"expert": at(plane, to)},
                ).start()

    def finish(t, s, x, gates, slot):
        drain(home_rx.at[t, s, blocks(0, 7)], recv.at[t, s, HOME])
        terms = []
        for e in range(4):
            two = home_rx[t, s, blocks(2 * e, 2)].astype(f32)
            sums = two[0:BLOCK] + two[BLOCK : 2 * BLOCK]
            for c in range(CAP):
                factor = jnp.where(slot[:, e : e + 1] == c, gates[:, e : e + 1], 0.0)
                terms.append((sums, c, factor))
        rows = []
        for q in range(QUARTERS):
            total = x[q]
            for sums, c, factor in terms:
                total = total + factor * sums[q * 4 + c : q * 4 + c + 1, :]
            rows.append(total)
        return rows

    rounds = [[sibling], y_mates, [{"expert": at(1 - zh, y)}], x_mates, z_mates]

    def mass_send(k):
        for i, device in enumerate(rounds[k]):
            pltpu.make_async_remote_copy(
                src_ref=mtx.at[k], dst_ref=mrx.at[k, i], send_sem=msend.at[k],
                recv_sem=mrecv.at[k], device_id=device, device_id_type=MESH,
            ).start()

    def mass_take(k):
        count = len(rounds[k])
        drain(mrx.at[k, pl.ds(0, count)], mrecv.at[k])
        return sum((mrx[k, i] for i in range(count)), mtx[k])

    def mass_step(k):
        mtx[k + 1] = mass_take(k)
        mass_send(k + 1)

    x = [first_rows(s) for s in range(2)]
    routed = [None, None]
    for s in range(2):
        normed4, gates, slot = route(x[s], picks[0, s], centroids[s])
        pack(0, s, normed4, slot)
        routed[s] = (gates, slot)
    pl.semaphore_wait(barrier, len(greeted))
    for s in range(2):
        dispatch(0, s)
    for s in range(2):
        send_weights(s)
    send_ahead_of_relay()
    masses = [jnp.sum(routed[s][0], axis=0, keepdims=True) for s in range(2)]
    for s in range(2):
        pass_on(0, s)
    for s in range(2):
        experts(0, s)
    for s in range(2):
        send_home(0, s)
    for s in range(2):
        rows = finish(0, s, x[s], *routed[s])
        rounded = jnp.concatenate(rows, axis=0).astype(bf16)
        xtx[s] = rounded
        if s == 0:
            for i in range(2):
                for j in range(2):
                    ref = (picks_next if j == 0 else centroids_next).at[i]
                    drain(ref, precv.at[i, j])
        normed4, _, slot = route(relayed_rows(xtx, s), picks_next[s], centroids_next[s])
        pack(1, s, normed4, slot)
        dispatch(1, s)
        remote(
            xtx.at[s], xr.at[s], 0, s, RELAY, {"pipe": ahead if s == 0 else behind}
        ).start()

    for s in range(2):
        pass_on(1, s)
    for s in range(2):
        drain(xr.at[s], recv.at[0, s, RELAY])
        x[s] = relayed_rows(xr, s)
        _, gates, slot = route(x[s], picks[1, s], centroids[s])
        routed[s] = (gates, slot)
        masses[s] = masses[s] + jnp.sum(gates, axis=0, keepdims=True)
    row = iota((16, 4), 0)
    mtx[0] = jnp.zeros_like(mtx[0])
    mtx[0, :, 0:4] = jnp.where(row == pipe, masses[0], 0.0) + jnp.where(
        row == SECTIONS - 1 - pipe, masses[1], 0.0
    )
    mass_send(0)
    for s in range(2):
        experts(1, s)
        mass_step(s)
    for s in range(2):
        send_home(1, s)
        mass_step(2 + s)
    for s in range(2):
        rows = finish(1, s, x[s], *routed[s])
        ref = out_a if s == 0 else out_b
        for q in range(QUARTERS):
            ref[0, :, q * quarter : (q + 1) * quarter] = rows[q].astype(bf16)
    out_load[...] = mass_take(4)[:, 0:4] / (2 * TICKS * 8 * 32)

    for s in range(2):
        for which in range(2):
            drain(half_of_weight(s, which), wsend.at[s, which])
        drain(picks_next.at[s], psend.at[s, 0])
        drain(centroids_next.at[s], psend.at[s, 1])
    for k in range(5):
        drain(mrx.at[k, pl.ds(0, len(rounds[k]))], msend.at[k])
    for s in range(2):
        drain(xr.at[s], send.at[0, s, RELAY])
        for t in range(TICKS):
            drain(rx.at[t, s, blocks(0, 3 + t)], send.at[t, s, TO_OWN])
            for kind in (TO_OTHER, ON_OWN, ON_OTHER, SWAP_OWN, SWAP_OTHER):
                drain(rx.at[t, s, blocks(0, 4)], send.at[t, s, kind])
            drain(home_rx.at[t, s, blocks(0, 7)], send.at[t, s, HOME])


def shards(stream_a, stream_b, routes, up_weight, down_weight, router_weight):
    features = stream_a.shape[2]
    quarter = features // QUARTERS
    vmem = pl.BlockSpec(memory_space=pltpu.VMEM)
    hbm = pl.BlockSpec(memory_space=pl.ANY)
    bf16, f32 = jnp.bfloat16, jnp.float32
    return pl.pallas_call(
        kernel,
        out_shape=(
            jax.ShapeDtypeStruct(stream_a.shape, bf16),
            jax.ShapeDtypeStruct(stream_b.shape, bf16),
            jax.ShapeDtypeStruct((16, 4), f32),
        ),
        in_specs=[vmem, vmem, vmem, vmem, hbm, hbm],
        out_specs=(vmem, vmem, vmem),
        scratch_shapes=[
            pltpu.VMEM((2, quarter, QUARTERS * 256), bf16),
            pltpu.VMEM((2, 256, features), bf16),
            pltpu.VMEM((TICKS, 2, 64, quarter), bf16),
            pltpu.VMEM((TICKS, 2, 256, quarter), bf16),
            pltpu.VMEM((2, 128, quarter), f32),
            pltpu.VMEM((TICKS, 2, 128, quarter), bf16),
            pltpu.VMEM((TICKS, 2, 128, quarter), bf16),
            pltpu.VMEM((TICKS, 2, 128, quarter), bf16),
            pltpu.VMEM((TICKS, 2, 128, quarter), bf16),
            pltpu.VMEM((2, 32, quarter), bf16),
            pltpu.VMEM((2, 32, quarter), bf16),
            pltpu.VMEM((TICKS, 2, 8, 128), f32),
            pltpu.VMEM((2, 8, 128), f32),
            pltpu.VMEM((2, 16, quarter), bf16),
            pltpu.VMEM((2, 16, quarter), bf16),
            pltpu.VMEM((5, 16, 128), f32),
            pltpu.VMEM((5, SIDE - 1, 16, 128), f32),
            pltpu.SemaphoreType.DMA((TICKS, 2, KINDS)),
            pltpu.SemaphoreType.DMA((TICKS, 2, KINDS)),
            pltpu.SemaphoreType.DMA((2, 2)),
            pltpu.SemaphoreType.DMA((2, 2)),
            pltpu.SemaphoreType.DMA((2, 2)),
            pltpu.SemaphoreType.DMA((2, 2)),
            pltpu.SemaphoreType.DMA((2, 2)),
            pltpu.SemaphoreType.DMA((5,)),
            pltpu.SemaphoreType.DMA((5,)),
        ],
        compiler_params=pltpu.CompilerParams(
            collective_id=0, has_side_effects=True, vmem_limit_bytes=60 * 2**20
        ),
        name="relay",
    )(
        stream_a, stream_b, jnp.swapaxes(routes, 3, 4), jnp.swapaxes(router_weight, 2, 3),
        up_weight, down_weight,
    )


def solution(mesh):
    return jax.shard_map(
        shards,
        mesh=mesh,
        in_specs=(
            P("pipe", "expert", None),
            P("pipe", "expert", None),
            P(None, None, "pipe", "expert", None),
            P(None, "pipe", None, "expert"),
            P(None, "pipe", "expert", None),
            P(None, "pipe", None, None),
        ),
        out_specs=(P("pipe", "expert", None), P("pipe", "expert", None), P()),
        check_vma=False,
    )
```

```python
import jax
import jax.numpy as jnp
from jax import lax
from jax.experimental import pallas as pl
from jax.experimental.pallas import tpu as pltpu
from jax.sharding import PartitionSpec as P

TICKS = 2
EPS = 1e-06
QUARTERS = 4
CAP = 4
SIDE = 8
SECTIONS = 16
BLOCK = 16
MESH = pl.DeviceIdType.MESH

TO_OWN, TO_OTHER, ON_OWN, ON_OTHER, SWAP_OWN, SWAP_OTHER, HOME, RELAY = range(8)
KINDS = 8


def kernel(
    sa, sb, routes_in, router_in, up, down,
    out_a, out_b, out_load,
    xin, routes, router, u, w, tx, rx, mine, swap_tx, swap_rx, home_tx, home_rx, xtx, xr,
    picks, picks_next, centroids, centroids_next, mtx, mrx,
    send, recv, inputs, wlocal, wsend, wrecv, psend, precv, msend, mrecv,
):
    quarter = u.shape[1]
    features = QUARTERS * quarter
    f32, bf16 = jnp.float32, jnp.bfloat16
    pipe = lax.axis_index("pipe")
    ex = lax.axis_index("expert")
    zh = ex // 16
    y = (ex // 2) % SIDE
    core = ex % 2
    turn = 1 - 2 * (y % 2)
    sibling = {"expert": ex + 1 - 2 * core}
    mate = {"expert": ex + 2 * turn}
    ahead = (pipe + 1) % SECTIONS
    behind = (pipe + SECTIONS - 1) % SECTIONS

    def at(plane, to):
        return plane * 16 + to * 2 + core

    targets = [(y + turn * step + SIDE) % SIDE for step in (0, -1, 2, -3)]
    sources = [(y - turn * k + SIDE) % SIDE for k in range(4)]

    px, pz = pipe % 4, pipe // 4
    x_mates = [{"pipe": pz * 4 + (px + k) % 4} for k in range(1, 4)]
    z_mates = [{"pipe": ((pz + k) % 4) * 4 + px} for k in range(1, 4)]

    def weight_parts(s, which):
        if which == 0:
            return [
                (
                    up.at[s, 0, pl.ds(q * quarter, quarter), :],
                    u.at[s, :, pl.ds(pl.multiple_of(q * 256 + core * 128, 128), 128)],
                )
                for q in range(QUARTERS)
            ]
        return [(down.at[s, 0], w.at[s, pl.ds(pl.multiple_of(core * 128, 128), 128), :])]

    barrier = pltpu.get_barrier_semaphore()

    def greet(device):
        pl.semaphore_signal(barrier, inc=1, device_id=device, device_id_type=MESH)

    near = [(y + step + SIDE) % SIDE for step in (2, -2)] + [
        (y + turn * step + SIDE) % SIDE for step in (-1, -3)
    ]
    greeted = [{"expert": at(1 - zh, to)} for to in near + [y]]
    greeted += [{"expert": at(zh, to)} for to in near] + [{"pipe": ahead}, {"pipe": behind}]
    greeted += x_mates + z_mates + [mate, sibling]
    for device in greeted:
        greet(device)

    input_copies = [
        pltpu.make_async_copy(src, dst, inputs.at[i])
        for i, (src, dst) in enumerate(
            (
                (sa.at[0], xin.at[0]),
                (sb.at[0], xin.at[1]),
                (routes_in, routes),
                (router_in, router),
            )
        )
    ]
    for copy in input_copies:
        copy.start()
    for s in range(2):
        for which in range(2):
            for src, dst in weight_parts(s, which):
                pltpu.make_async_copy(src, dst, wlocal.at[s, which]).start()

    def remote(src, dst, t, s, kind, device):
        return pltpu.make_async_remote_copy(
            src_ref=src, dst_ref=dst, send_sem=send.at[t, s, kind],
            recv_sem=recv.at[t, s, kind], device_id=device, device_id_type=MESH,
        )

    def drain(ref, sem):
        pltpu.make_async_copy(ref, ref, sem).wait()

    def half_of_weight(s, which):
        return u.at[s, :, pl.ds(0, 512)] if which == 0 else w.at[s, pl.ds(0, 128), :]

    def send_weights(s):
        for which in range(2):
            for src, dst in weight_parts(s, which):
                pltpu.make_async_remote_copy(
                    src_ref=src, dst_ref=dst, send_sem=wsend.at[s, which],
                    recv_sem=wrecv.at[s, which], device_id=sibling, device_id_type=MESH,
                ).start()

    def iota(shape, dim):
        return lax.broadcasted_iota(jnp.int32, shape, dim)

    def across(a, b):
        return lax.dot_general(a, b, (((1,), (1,)), ((), ())), preferred_element_type=f32)

    lane4 = iota((8, 4), 1).astype(f32)
    low8 = (iota((8, 8), 0) > iota((8, 8), 1)).astype(bf16)
    eye8 = (iota((8, 8), 0) == iota((8, 8), 1)).astype(bf16)
    expert_hot = (iota((64, 4), 0) // BLOCK == iota((64, 4), 1)).astype(bf16)
    row_t, col_t = iota((64, 32), 0), iota((64, 32), 1)
    same_quarter = (row_t // 4) % 4 == col_t // 8
    slot_t = (row_t % 4).astype(f32)

    for copy in input_copies:
        copy.wait()

    for s in range(2):
        for t in range(TICKS):
            picks[t, s, :, 0:2] = across(eye8, routes[t, s, 0].astype(f32).astype(bf16))
        centroids[s] = jnp.concatenate(
            [
                router[s, 0, :, q * quarter : (q + 1) * quarter].astype(f32)
                for q in range(QUARTERS)
            ],
            axis=0,
        ).astype(bf16)

    def send_ahead_of_relay():
        for s, section in ((0, behind), (1, ahead)):
            for i, (src, dst) in enumerate(
                ((picks.at[1, s], picks_next.at[s]), (centroids.at[s], centroids_next.at[s]))
            ):
                pltpu.make_async_remote_copy(
                    src_ref=src, dst_ref=dst, send_sem=psend.at[s, i], recv_sem=precv.at[s, i],
                    device_id={"pipe": section}, device_id_type=MESH,
                ).start()

    def first_rows(s):
        return [
            xin[s, :, q * quarter : (q + 1) * quarter].astype(f32) for q in range(QUARTERS)
        ]

    def relayed_rows(ref, s):
        rows = ref[s].astype(f32)
        return [rows[q * 8 : (q + 1) * 8] for q in range(QUARTERS)]

    def route(x, picked, central):
        total = sum(jnp.sum(part * part, axis=1, keepdims=True) for part in x)
        scale = lax.rsqrt(total / features + EPS)
        normed4 = jnp.concatenate([part * scale for part in x], axis=0).astype(bf16)
        mixed = across(normed4, central)
        logits = sum(
            mixed[q * 8 : (q + 1) * 8, q * 4 : (q + 1) * 4] for q in range(QUARTERS)
        )
        affinity = jax.nn.sigmoid(logits)
        member = [(picked[:, j : j + 1] == lane4).astype(f32) for j in range(2)]
        chosen = [jnp.sum(m * affinity, axis=1, keepdims=True) for m in member]
        both = chosen[0] + chosen[1]
        gates = (chosen[0] / both) * member[0] + (chosen[1] / both) * member[1]
        selected = member[0] + member[1]
        before = jnp.dot(low8, selected.astype(bf16), preferred_element_type=f32)
        slot = jnp.where(selected > 0, before, -1.0)
        return normed4, gates, slot

    def pack(t, s, normed4, slot):
        slot_of = across(expert_hot, jnp.concatenate([slot] * QUARTERS, axis=0).astype(bf16))
        place = jnp.where(same_quarter & (slot_of == slot_t), 1.0, 0.0).astype(bf16)
        tx[t, s] = jnp.dot(place, normed4, preferred_element_type=f32).astype(bf16)

    def block(index):
        if isinstance(index, int):
            return pl.ds(index * BLOCK, BLOCK)
        return pl.ds(pl.multiple_of(index * BLOCK, BLOCK), BLOCK)

    def blocks(first, count):
        return pl.ds(first * BLOCK, count * BLOCK)

    def dispatch(t, s):
        for plane, kind, base in ((zh, TO_OWN, 0), (1 - zh, TO_OTHER, 4)):
            for k, to in reversed(list(enumerate(targets))):
                src = block(plane * 2 + to // 4)
                if t == 0 and base == 0 and k == 0:
                    rx[t, s, block(0)] = tx[t, s, src]
                    continue
                device = {"expert": at(plane, to)}
                if t > 0:
                    device["pipe"] = ahead if s == 0 else behind
                remote(
                    tx.at[t, s, src], rx.at[t, s, block(base + k)], t, s, kind, device
                ).start()

    def pass_on(t, s, group=None):
        if group is None:
            pass_on(t, s, 0)
            pass_on(t, s, 1)
            return
        own = blocks(1, 3) if t == 0 else blocks(0, 4)
        if group == 1:
            drain(rx.at[t, s, blocks(4, 4)], recv.at[t, s, TO_OTHER])
            remote(rx.at[t, s, blocks(4, 4)], rx.at[t, s, blocks(12, 4)], t, s, ON_OTHER, mate).start()
            return
        drain(rx.at[t, s, own], recv.at[t, s, TO_OWN])
        remote(rx.at[t, s, blocks(0, 4)], rx.at[t, s, blocks(8, 4)], t, s, ON_OWN, mate).start()

    def experts(t, s):
        drain(rx.at[t, s, blocks(8, 4)], recv.at[t, s, ON_OWN])
        drain(rx.at[t, s, blocks(12, 4)], recv.at[t, s, ON_OTHER])
        if t == 0:
            drain(half_of_weight(s, 0), wlocal.at[s, 0])
            drain(half_of_weight(s, 0), wrecv.at[s, 0])
        arrived = rx[t, s]
        lower = iota((16, 8, 256), 1) < 4
        lifted = [
            jnp.dot(
                arrived, u[s, :, q * 256 : (q + 1) * 256], preferred_element_type=f32
            ).reshape(16, 2, 8, 256)
            for q in range(QUARTERS)
        ]
        part = jnp.where(lower, lifted[0][:, 0], lifted[1][:, 0]) + jnp.where(
            lower, lifted[2][:, 1], lifted[3][:, 1]
        )
        part = part.reshape(128, 256)
        lower2 = iota((128, 256), 0) % 8 < 4
        other = jnp.where(lower2, pltpu.roll(part, 124, 0), pltpu.roll(part, 4, 0))
        hidden = jax.nn.silu(part + other).astype(bf16)
        if t == 0:
            drain(half_of_weight(s, 1), wlocal.at[s, 1])
            drain(half_of_weight(s, 1), wrecv.at[s, 1])
        lower3 = iota((128, quarter), 0) % 8 < 4
        halves = []
        for h in range(2):
            two = [
                jnp.dot(
                    hidden, w[s, :, q * quarter : (q + 1) * quarter], preferred_element_type=f32
                )
                for q in (2 * h, 2 * h + 1)
            ]
            halves.append(jnp.where(lower3, two[0], two[1]).reshape(16, 1, 8, quarter))
        both = jnp.concatenate(halves, axis=1).reshape(256, quarter)
        mine[s] = both[0:128]
        swap_tx[t, s] = both[128:256].astype(bf16)
        for kind, first in ((SWAP_OTHER, 4), (SWAP_OWN, 0)):
            remote(
                swap_tx.at[t, s, blocks(first, 4)], swap_rx.at[t, s, blocks(first, 4)],
                t, s, kind, mate,
            ).start()

    def send_home(t, s):
        slot = zh * 4 + y // 2
        for plane, kind, base in ((1 - zh, SWAP_OTHER, 4), (zh, SWAP_OWN, 0)):
            rows = blocks(base, 4)
            drain(swap_rx.at[t, s, rows], recv.at[t, s, kind])
            home_tx[t, s, rows] = (mine[s, rows] + swap_rx[t, s, rows].astype(f32)).astype(bf16)
            for k, to in reversed(list(enumerate(sources))):
                if base == 0 and k == 0:
                    home_rx[t, s, block(slot)] = home_tx[t, s, block(0)]
                    continue
                remote(
                    home_tx.at[t, s, block(base + k)], home_rx.at[t, s, block(slot)],
                    t, s, HOME, {"expert": at(plane, to)},
                ).start()

    def finish(t, s, x, gates, slot):
        drain(home_rx.at[t, s, blocks(0, 7)], recv.at[t, s, HOME])
        terms = []
        for e in range(4):
            two = home_rx[t, s, blocks(2 * e, 2)].astype(f32)
            sums = two[0:BLOCK] + two[BLOCK : 2 * BLOCK]
            for c in range(CAP):
                factor = jnp.where(slot[:, e : e + 1] == c, gates[:, e : e + 1], 0.0)
                terms.append((sums, c, factor))
        rows = []
        for q in range(QUARTERS):
            total = x[q]
            for sums, c, factor in terms:
                total = total + factor * sums[q * 4 + c : q * 4 + c + 1, :]
            rows.append(total)
        return rows

    spread = [{"expert": at(zh, to)} for to in targets[1:]]
    spread += [{"expert": at(1 - zh, to)} for to in targets]
    rounds = [[sibling], spread, [mate], x_mates, z_mates]

    def mass_send(k):
        for i, device in enumerate(rounds[k]):
            pltpu.make_async_remote_copy(
                src_ref=mtx.at[k], dst_ref=mrx.at[k, i], send_sem=msend.at[k],
                recv_sem=mrecv.at[k], device_id=device, device_id_type=MESH,
            ).start()

    def mass_take(k):
        count = len(rounds[k])
        drain(mrx.at[k, pl.ds(0, count)], mrecv.at[k])
        return sum((mrx[k, i] for i in range(count)), mtx[k])

    def mass_step(k):
        mtx[k + 1] = mass_take(k)
        mass_send(k + 1)

    x = [first_rows(s) for s in range(2)]
    routed = [None, None]
    for s in range(2):
        normed4, gates, slot = route(x[s], picks[0, s], centroids[s])
        pack(0, s, normed4, slot)
        routed[s] = (gates, slot)
    pl.semaphore_wait(barrier, len(greeted))
    for s in range(2):
        dispatch(0, s)
    for s in range(2):
        send_weights(s)
    send_ahead_of_relay()
    row = iota((16, 4), 0)

    def mass_rows(gates, layer):
        return jnp.where(row == layer, jnp.sum(gates, axis=0, keepdims=True), 0.0)

    masses = mass_rows(routed[0][0], pipe) + mass_rows(routed[1][0], SECTIONS - 1 - pipe)
    for g in range(2):
        for s in range(2):
            pass_on(0, s, g)
    for s in range(2):
        experts(0, s)
    for s in range(2):
        send_home(0, s)
    for i in range(2):
        drain(picks_next.at[i], precv.at[i, 0])
        drain(centroids_next.at[i], precv.at[i, 1])
    for s in range(2):
        rows = finish(0, s, x[s], *routed[s])
        xtx[s] = jnp.concatenate(rows, axis=0).astype(bf16)
        normed4, gates, slot = route(relayed_rows(xtx, s), picks_next[s], centroids_next[s])
        pack(1, s, normed4, slot)
        dispatch(1, s)
        remote(
            xtx.at[s], xr.at[s], 0, s, RELAY, {"pipe": ahead if s == 0 else behind}
        ).start()
        masses = masses + mass_rows(gates, ahead if s == 0 else SECTIONS - 1 - behind)
    mtx[0] = jnp.zeros_like(mtx[0])
    mtx[0, :, 0:4] = masses
    mass_send(0)

    pass_on(1, 0, 0)
    mass_step(0)
    pass_on(1, 1, 0)
    pass_on(1, 0, 1)
    pass_on(1, 1, 1)
    for s in range(2):
        drain(xr.at[s], recv.at[0, s, RELAY])
        x[s] = relayed_rows(xr, s)
        _, gates, slot = route(x[s], picks[1, s], centroids[s])
        routed[s] = (gates, slot)
    experts(1, 0)
    mass_step(1)
    experts(1, 1)
    mass_step(2)
    send_home(1, 0)
    send_home(1, 1)
    mass_step(3)
    for s in range(2):
        rows = finish(1, s, x[s], *routed[s])
        ref = out_a if s == 0 else out_b
        for q in range(QUARTERS):
            ref[0, :, q * quarter : (q + 1) * quarter] = rows[q].astype(bf16)
    out_load[...] = mass_take(4)[:, 0:4] / (2 * TICKS * 8 * 32)

    for s in range(2):
        for which in range(2):
            drain(half_of_weight(s, which), wsend.at[s, which])
        drain(picks_next.at[s], psend.at[s, 0])
        drain(centroids_next.at[s], psend.at[s, 1])
    for k in range(5):
        drain(mrx.at[k, pl.ds(0, len(rounds[k]))], msend.at[k])
    for s in range(2):
        drain(xr.at[s], send.at[0, s, RELAY])
        for t in range(TICKS):
            drain(rx.at[t, s, blocks(0, 3 + t)], send.at[t, s, TO_OWN])
            for kind in (TO_OTHER, ON_OWN, ON_OTHER, SWAP_OWN, SWAP_OTHER):
                drain(rx.at[t, s, blocks(0, 4)], send.at[t, s, kind])
            drain(home_rx.at[t, s, blocks(0, 7)], send.at[t, s, HOME])


def hand_over(a, b, load, out_a, out_b, out_load):
    out_a[...] = a[...]
    out_b[...] = b[...]
    out_load[...] = load[...].T


def shards(stream_a, stream_b, routes, up_weight, down_weight, router_weight):
    features = stream_a.shape[2]
    quarter = features // QUARTERS
    vmem = pl.BlockSpec(memory_space=pltpu.VMEM)
    hbm = pl.BlockSpec(memory_space=pltpu.HBM)
    bf16, f32 = jnp.bfloat16, jnp.float32
    results = pl.pallas_call(
        kernel,
        out_shape=(
            jax.ShapeDtypeStruct(stream_a.shape, bf16),
            jax.ShapeDtypeStruct(stream_b.shape, bf16),
            jax.ShapeDtypeStruct((16, 4), f32),
        ),
        in_specs=[hbm] * 6,
        out_specs=(vmem, vmem, vmem),
        scratch_shapes=[
            pltpu.VMEM((2, 8, features), bf16),
            pltpu.VMEM((TICKS, 2, 1, 2, 8), jnp.int32),
            pltpu.VMEM((2, 1, 4, features), bf16),
            pltpu.VMEM((2, quarter, QUARTERS * 256), bf16),
            pltpu.VMEM((2, 256, features), bf16),
            pltpu.VMEM((TICKS, 2, 64, quarter), bf16),
            pltpu.VMEM((TICKS, 2, 256, quarter), bf16),
            pltpu.VMEM((2, 128, quarter), f32),
            pltpu.VMEM((TICKS, 2, 128, quarter), bf16),
            pltpu.VMEM((TICKS, 2, 128, quarter), bf16),
            pltpu.VMEM((TICKS, 2, 128, quarter), bf16),
            pltpu.VMEM((TICKS, 2, 128, quarter), bf16),
            pltpu.VMEM((2, 32, quarter), bf16),
            pltpu.VMEM((2, 32, quarter), bf16),
            pltpu.VMEM((TICKS, 2, 8, 128), f32),
            pltpu.VMEM((2, 8, 128), f32),
            pltpu.VMEM((2, 16, quarter), bf16),
            pltpu.VMEM((2, 16, quarter), bf16),
            pltpu.VMEM((5, 16, 128), f32),
            pltpu.VMEM((5, SIDE - 1, 16, 128), f32),
            pltpu.SemaphoreType.DMA((TICKS, 2, KINDS)),
            pltpu.SemaphoreType.DMA((TICKS, 2, KINDS)),
            pltpu.SemaphoreType.DMA((4,)),
            pltpu.SemaphoreType.DMA((2, 2)),
            pltpu.SemaphoreType.DMA((2, 2)),
            pltpu.SemaphoreType.DMA((2, 2)),
            pltpu.SemaphoreType.DMA((2, 2)),
            pltpu.SemaphoreType.DMA((2, 2)),
            pltpu.SemaphoreType.DMA((5,)),
            pltpu.SemaphoreType.DMA((5,)),
        ],
        compiler_params=pltpu.CompilerParams(
            collective_id=0, has_side_effects=True, vmem_limit_bytes=55 * 2**20
        ),
        name="relay",
    )(
        stream_a, stream_b, jnp.swapaxes(routes, 3, 4), jnp.swapaxes(router_weight, 2, 3),
        up_weight, down_weight,
    )
    final_a, final_b, load = pl.pallas_call(
        hand_over,
        out_shape=(
            jax.ShapeDtypeStruct(stream_a.shape, bf16),
            jax.ShapeDtypeStruct(stream_b.shape, bf16),
            jax.ShapeDtypeStruct((4, 16), f32),
        ),
        in_specs=[vmem] * 3,
        out_specs=(vmem,) * 3,
        compiler_params=pltpu.CompilerParams(vmem_limit_bytes=55 * 2**20),
        name="hand_over",
    )(*results)
    return final_a, final_b, load.T


def solution(mesh):
    return jax.shard_map(
        shards,
        mesh=mesh,
        in_specs=(
            P("pipe", "expert", None),
            P("pipe", "expert", None),
            P(None, None, "pipe", "expert", None),
            P(None, "pipe", None, "expert"),
            P(None, "pipe", "expert", None),
            P(None, "pipe", None, None),
        ),
        out_specs=(P("pipe", "expert", None), P("pipe", "expert", None), P()),
        check_vma=False,
    )
```

```python
import jax
import jax.numpy as jnp
from jax import lax
from jax.experimental import pallas as pl
from jax.experimental.pallas import tpu as pltpu
from jax.sharding import PartitionSpec as P

TICKS = 2
EPS = 1e-06
QUARTERS = 4
CAP = 4
SIDE = 8
SECTIONS = 16
BLOCK = 16
MESH = pl.DeviceIdType.MESH

TO_OWN, TO_OTHER, ON_OWN, ON_OTHER, SWAP_OWN, SWAP_OTHER, HOME, RELAY = range(8)
TO_OTHER_FAR = 8
KINDS = 9


def kernel(
    sa, sb, routes_in, router_in, up, down,
    out_a, out_b, out_load,
    xin, routes, router, u, w, tx, rx, mine, swap_tx, swap_rx, home_tx, home_rx, xtx, xr,
    picks, picks_next, centroids, centroids_next, mtx, mrx,
    send, recv, inputs, wlocal, wsend, wrecv, psend, precv, msend, mrecv,
):
    quarter = u.shape[1]
    features = QUARTERS * quarter
    f32, bf16 = jnp.float32, jnp.bfloat16
    pipe = lax.axis_index("pipe")
    ex = lax.axis_index("expert")
    zh = ex // 16
    y = (ex // 2) % SIDE
    core = ex % 2
    turn = 1 - 2 * (y % 2)
    sibling = {"expert": ex + 1 - 2 * core}
    mate = {"expert": ex + 2 * turn}
    ahead = (pipe + 1) % SECTIONS
    behind = (pipe + SECTIONS - 1) % SECTIONS

    def at(plane, to):
        return plane * 16 + to * 2 + core

    targets = [(y + turn * step + SIDE) % SIDE for step in (0, -1, 2, -3)]
    sources = [(y - turn * k + SIDE) % SIDE for k in range(4)]

    px, pz = pipe % 4, pipe // 4
    x_mates = [{"pipe": pz * 4 + (px + k) % 4} for k in range(1, 4)]
    z_mates = [{"pipe": ((pz + k) % 4) * 4 + px} for k in range(1, 4)]

    def weight_parts(s, which):
        if which == 0:
            return [
                (
                    up.at[s, 0, pl.ds(q * quarter, quarter), :],
                    u.at[s, :, pl.ds(pl.multiple_of(q * 256 + core * 128, 128), 128)],
                )
                for q in range(QUARTERS)
            ]
        return [(down.at[s, 0], w.at[s, pl.ds(pl.multiple_of(core * 128, 128), 128), :])]

    barrier = pltpu.get_barrier_semaphore()

    def greet(device):
        pl.semaphore_signal(barrier, inc=1, device_id=device, device_id_type=MESH)

    near = [(y + step + SIDE) % SIDE for step in (2, -2)] + [
        (y + turn * step + SIDE) % SIDE for step in (-1, -3)
    ]
    greeted = [{"expert": at(1 - zh, to)} for to in near + [y]]
    greeted += [{"expert": at(zh, to)} for to in near] + [{"pipe": ahead}, {"pipe": behind}]
    greeted += x_mates + z_mates + [mate, sibling]
    for device in greeted:
        greet(device)

    input_copies = [
        pltpu.make_async_copy(src, dst, inputs.at[i])
        for i, (src, dst) in enumerate(
            (
                (sa.at[0], xin.at[0]),
                (sb.at[0], xin.at[1]),
                (routes_in, routes),
                (router_in, router),
            )
        )
    ]
    for copy in input_copies:
        copy.start()
    for s in range(2):
        for which in range(2):
            for src, dst in weight_parts(s, which):
                pltpu.make_async_copy(src, dst, wlocal.at[s, which]).start()

    def remote(src, dst, t, s, kind, device):
        return pltpu.make_async_remote_copy(
            src_ref=src, dst_ref=dst, send_sem=send.at[t, s, kind],
            recv_sem=recv.at[t, s, kind], device_id=device, device_id_type=MESH,
        )

    def drain(ref, sem):
        pltpu.make_async_copy(ref, ref, sem).wait()

    def half_of_weight(s, which):
        return u.at[s, :, pl.ds(0, 512)] if which == 0 else w.at[s, pl.ds(0, 128), :]

    def send_weights(s, which):
        for src, dst in weight_parts(s, which):
            pltpu.make_async_remote_copy(
                src_ref=src, dst_ref=dst, send_sem=wsend.at[s, which],
                recv_sem=wrecv.at[s, which], device_id=sibling, device_id_type=MESH,
            ).start()

    def iota(shape, dim):
        return lax.broadcasted_iota(jnp.int32, shape, dim)

    def across(a, b):
        return lax.dot_general(a, b, (((1,), (1,)), ((), ())), preferred_element_type=f32)

    lane4 = iota((8, 4), 1).astype(f32)
    low8 = (iota((8, 8), 0) > iota((8, 8), 1)).astype(bf16)
    eye8 = (iota((8, 8), 0) == iota((8, 8), 1)).astype(bf16)
    expert_hot = (iota((64, 4), 0) // BLOCK == iota((64, 4), 1)).astype(bf16)
    row_t, col_t = iota((64, 32), 0), iota((64, 32), 1)
    same_quarter = (row_t // 4) % 4 == col_t // 8
    slot_t = (row_t % 4).astype(f32)

    for copy in input_copies:
        copy.wait()

    for s in range(2):
        for t in range(TICKS):
            picks[t, s, :, 0:2] = across(eye8, routes[t, s, 0].astype(f32).astype(bf16))
        centroids[s] = jnp.concatenate(
            [
                router[s, 0, :, q * quarter : (q + 1) * quarter].astype(f32)
                for q in range(QUARTERS)
            ],
            axis=0,
        ).astype(bf16)

    def send_ahead_of_relay():
        for s, section in ((0, behind), (1, ahead)):
            for i, (src, dst) in enumerate(
                ((picks.at[1, s], picks_next.at[s]), (centroids.at[s], centroids_next.at[s]))
            ):
                pltpu.make_async_remote_copy(
                    src_ref=src, dst_ref=dst, send_sem=psend.at[s, i], recv_sem=precv.at[s, i],
                    device_id={"pipe": section}, device_id_type=MESH,
                ).start()

    def first_rows(s):
        return [
            xin[s, :, q * quarter : (q + 1) * quarter].astype(f32) for q in range(QUARTERS)
        ]

    def relayed_rows(ref, s):
        rows = ref[s].astype(f32)
        return [rows[q * 8 : (q + 1) * 8] for q in range(QUARTERS)]

    def seats(picked):
        member = [(picked[:, j : j + 1] == lane4).astype(f32) for j in range(2)]
        selected = member[0] + member[1]
        before = jnp.dot(low8, selected.astype(bf16), preferred_element_type=f32)
        slot = jnp.where(selected > 0, before, -1.0)
        return member, slot

    def placing(slot):
        slot_of = across(expert_hot, jnp.concatenate([slot] * QUARTERS, axis=0).astype(bf16))
        return jnp.where(same_quarter & (slot_of == slot_t), 1.0, 0.0).astype(bf16)

    def normalize(x):
        total = sum(jnp.sum(part * part, axis=1, keepdims=True) for part in x)
        scale = lax.rsqrt(total / features + EPS)
        return jnp.concatenate([part * scale for part in x], axis=0).astype(bf16)

    def gating(normed4, member, central):
        mixed = across(normed4, central)
        logits = sum(
            mixed[q * 8 : (q + 1) * 8, q * 4 : (q + 1) * 4] for q in range(QUARTERS)
        )
        affinity = jax.nn.sigmoid(logits)
        chosen = [jnp.sum(m * affinity, axis=1, keepdims=True) for m in member]
        both = chosen[0] + chosen[1]
        return (chosen[0] / both) * member[0] + (chosen[1] / both) * member[1]

    def pack(t, s, normed4, place):
        tx[t, s] = jnp.dot(place, normed4, preferred_element_type=f32).astype(bf16)

    def block(index):
        if isinstance(index, int):
            return pl.ds(index * BLOCK, BLOCK)
        return pl.ds(pl.multiple_of(index * BLOCK, BLOCK), BLOCK)

    def blocks(first, count):
        return pl.ds(first * BLOCK, count * BLOCK)

    def dispatch(t, s):
        for plane, kind, base in ((zh, TO_OWN, 0), (1 - zh, TO_OTHER, 4)):
            for k, to in reversed(list(enumerate(targets))):
                src = block(plane * 2 + to // 4)
                if t == 0 and base == 0 and k == 0:
                    rx[t, s, block(0)] = tx[t, s, src]
                    continue
                device = {"expert": at(plane, to)}
                if t > 0:
                    device["pipe"] = ahead if s == 0 else behind
                by = TO_OTHER_FAR if base == 4 and k > 1 else kind
                remote(
                    tx.at[t, s, src], rx.at[t, s, block(base + k)], t, s, by, device
                ).start()

    def pass_on(t, s, group):
        if group == 1:
            for kind, first in ((TO_OTHER_FAR, 6), (TO_OTHER, 4)):
                drain(rx.at[t, s, blocks(first, 2)], recv.at[t, s, kind])
                remote(
                    rx.at[t, s, blocks(first, 2)], rx.at[t, s, blocks(8 + first, 2)],
                    t, s, ON_OTHER, mate,
                ).start()
            return
        got = blocks(1, 3) if t == 0 else blocks(0, 4)
        drain(rx.at[t, s, got], recv.at[t, s, TO_OWN + group])
        remote(
            rx.at[t, s, blocks(group * 4, 4)], rx.at[t, s, blocks(8 + group * 4, 4)],
            t, s, ON_OWN + group, mate,
        ).start()

    def experts(t, s):
        drain(rx.at[t, s, blocks(8, 4)], recv.at[t, s, ON_OWN])
        drain(rx.at[t, s, blocks(12, 4)], recv.at[t, s, ON_OTHER])
        if t == 0:
            drain(half_of_weight(s, 0), wlocal.at[s, 0])
            drain(half_of_weight(s, 0), wrecv.at[s, 0])
        arrived = rx[t, s]
        lower = iota((16, 8, 256), 1) < 4
        lifted = [
            jnp.dot(
                arrived, u[s, :, q * 256 : (q + 1) * 256], preferred_element_type=f32
            ).reshape(16, 2, 8, 256)
            for q in range(QUARTERS)
        ]
        part = jnp.where(lower, lifted[0][:, 0], lifted[1][:, 0]) + jnp.where(
            lower, lifted[2][:, 1], lifted[3][:, 1]
        )
        part = part.reshape(128, 256)
        lower2 = iota((128, 256), 0) % 8 < 4
        other = jnp.where(lower2, pltpu.roll(part, 124, 0), pltpu.roll(part, 4, 0))
        hidden = jax.nn.silu(part + other).astype(bf16)
        if t == 0:
            drain(half_of_weight(s, 1), wlocal.at[s, 1])
            drain(half_of_weight(s, 1), wrecv.at[s, 1])
        lower3 = iota((128, quarter), 0) % 8 < 4
        halves = []
        for h in range(2):
            two = [
                jnp.dot(
                    hidden, w[s, :, q * quarter : (q + 1) * quarter], preferred_element_type=f32
                )
                for q in (2 * h, 2 * h + 1)
            ]
            halves.append(jnp.where(lower3, two[0], two[1]).reshape(16, 1, 8, quarter))
        both = jnp.concatenate(halves, axis=1).reshape(256, quarter)
        mine[s] = both[0:128]
        swap_tx[t, s] = both[128:256].astype(bf16)
        swap(t, s, 1)

    def swap(t, s, group):
        rows = blocks(group * 4, 4)
        remote(
            swap_tx.at[t, s, rows], swap_rx.at[t, s, rows], t, s, SWAP_OWN + group, mate
        ).start()

    def send_home(t, s, group):
        slot = zh * 4 + y // 2
        plane = 1 - zh if group else zh
        rows = blocks(group * 4, 4)
        drain(swap_rx.at[t, s, rows], recv.at[t, s, SWAP_OWN + group])
        home_tx[t, s, rows] = (mine[s, rows] + swap_rx[t, s, rows].astype(f32)).astype(bf16)
        for k, to in reversed(list(enumerate(sources))):
            if group == 0 and k == 0:
                home_rx[t, s, block(slot)] = home_tx[t, s, block(0)]
                continue
            remote(
                home_tx.at[t, s, block(group * 4 + k)], home_rx.at[t, s, block(slot)],
                t, s, HOME, {"expert": at(plane, to)},
            ).start()

    def finish(t, s, x, gates, slot):
        drain(home_rx.at[t, s, blocks(0, 7)], recv.at[t, s, HOME])
        terms = []
        for e in range(4):
            two = home_rx[t, s, blocks(2 * e, 2)].astype(f32)
            sums = two[0:BLOCK] + two[BLOCK : 2 * BLOCK]
            for c in range(CAP):
                factor = jnp.where(slot[:, e : e + 1] == c, gates[:, e : e + 1], 0.0)
                terms.append((sums, c, factor))
        rows = []
        for q in range(QUARTERS):
            total = x[q]
            for sums, c, factor in terms:
                total = total + factor * sums[q * 4 + c : q * 4 + c + 1, :]
            rows.append(total)
        return rows

    spread = [{"expert": at(zh, to)} for to in targets[1:]]
    spread += [{"expert": at(1 - zh, to)} for to in targets]
    rounds = [[sibling], spread, [mate], x_mates, z_mates]

    def mass_send(k):
        for i, device in enumerate(rounds[k]):
            pltpu.make_async_remote_copy(
                src_ref=mtx.at[k], dst_ref=mrx.at[k, i], send_sem=msend.at[k],
                recv_sem=mrecv.at[k], device_id=device, device_id_type=MESH,
            ).start()

    def mass_take(k):
        count = len(rounds[k])
        drain(mrx.at[k, pl.ds(0, count)], mrecv.at[k])
        return sum((mrx[k, i] for i in range(count)), mtx[k])

    def mass_step(k):
        mtx[k + 1] = mass_take(k)
        mass_send(k + 1)

    x = [first_rows(s) for s in range(2)]
    routed = [None, None]
    seated = [[seats(picks[t, s]) for s in range(2)] for t in range(TICKS)]
    for s in range(2):
        normed4 = normalize(x[s])
        member, slot = seated[0][s]
        pack(0, s, normed4, placing(slot))
        routed[s] = (gating(normed4, member, centroids[s]), slot)
    pl.semaphore_wait(barrier, len(greeted))
    row = iota((16, 4), 0)

    def mass_rows(gates, layer):
        return jnp.where(row == layer, jnp.sum(gates, axis=0, keepdims=True), 0.0)

    masses = [mass_rows(routed[0][0], pipe) + mass_rows(routed[1][0], SECTIONS - 1 - pipe)]

    def first(s):
        dispatch(0, s)
        if s == 1:
            send_ahead_of_relay()

    next_seats = [None, None]

    def look_ahead(s):
        drain(picks_next.at[s], precv.at[s, 0])
        drain(centroids_next.at[s], precv.at[s, 1])
        member, slot = seats(picks_next[s])
        next_seats[s] = (member, placing(slot))

    def between(s):
        xtx[s] = jnp.concatenate(finish(0, s, x[s], *routed[s]), axis=0).astype(bf16)
        normed4 = normalize(relayed_rows(xtx, s))
        member, place = next_seats[s]
        pack(1, s, normed4, place)
        dispatch(1, s)
        remote(
            xtx.at[s], xr.at[s], 0, s, RELAY, {"pipe": ahead if s == 0 else behind}
        ).start()
        gates = gating(normed4, member, centroids_next[s])
        masses.append(mass_rows(gates, ahead if s == 0 else SECTIONS - 1 - behind))

    def mass_start():
        mtx[0] = jnp.zeros_like(mtx[0])
        mtx[0, :, 0:4] = sum(masses)
        mass_send(0)

    def again(s):
        drain(xr.at[s], recv.at[0, s, RELAY])
        x[s] = relayed_rows(xr, s)
        member, slot = seated[1][s]
        routed[s] = (gating(normalize(x[s]), member, centroids[s]), slot)

    def last(s):
        rows = finish(1, s, x[s], *routed[s])
        ref = out_a if s == 0 else out_b
        for q in range(QUARTERS):
            ref[0, :, q * quarter : (q + 1) * quarter] = rows[q].astype(bf16)

    first(0)
    first(1)
    send_weights(0, 0)
    send_weights(0, 1)
    send_weights(1, 0)
    send_weights(1, 1)
    pass_on(0, 0, 0)
    pass_on(0, 1, 0)
    pass_on(0, 0, 1)
    pass_on(0, 1, 1)
    experts(0, 0)
    experts(0, 1)
    swap(0, 0, 0)
    swap(0, 1, 0)
    look_ahead(0)
    look_ahead(1)
    send_home(0, 0, 1)
    send_home(0, 1, 1)
    send_home(0, 0, 0)
    send_home(0, 1, 0)
    between(0)
    between(1)
    mass_start()
    pass_on(1, 0, 0)
    mass_step(0)
    pass_on(1, 1, 0)
    pass_on(1, 0, 1)
    pass_on(1, 1, 1)
    again(0)
    again(1)
    experts(1, 0)
    mass_step(1)
    experts(1, 1)
    swap(1, 0, 0)
    swap(1, 1, 0)
    mass_step(2)
    send_home(1, 0, 1)
    send_home(1, 1, 1)
    send_home(1, 0, 0)
    send_home(1, 1, 0)
    mass_step(3)
    last(0)
    last(1)
    out_load[...] = mass_take(4)[:, 0:4] / (2 * TICKS * 8 * 32)

    for s in range(2):
        for which in range(2):
            drain(half_of_weight(s, which), wsend.at[s, which])
        drain(picks_next.at[s], psend.at[s, 0])
        drain(centroids_next.at[s], psend.at[s, 1])
    for k in range(5):
        drain(mrx.at[k, pl.ds(0, len(rounds[k]))], msend.at[k])
    for s in range(2):
        drain(xr.at[s], send.at[0, s, RELAY])
        for t in range(TICKS):
            drain(rx.at[t, s, blocks(0, 3 + t)], send.at[t, s, TO_OWN])
            for kind in (TO_OTHER, TO_OTHER_FAR):
                drain(rx.at[t, s, blocks(0, 2)], send.at[t, s, kind])
            for kind in (ON_OWN, ON_OTHER, SWAP_OWN, SWAP_OTHER):
                drain(rx.at[t, s, blocks(0, 4)], send.at[t, s, kind])
            drain(home_rx.at[t, s, blocks(0, 7)], send.at[t, s, HOME])


def hand_over(a, b, load, out_a, out_b, out_load):
    out_a[...] = a[...]
    out_b[...] = b[...]
    out_load[...] = load[...].T


def shards(stream_a, stream_b, routes, up_weight, down_weight, router_weight):
    features = stream_a.shape[2]
    quarter = features // QUARTERS
    vmem = pl.BlockSpec(memory_space=pltpu.VMEM)
    hbm = pl.BlockSpec(memory_space=pltpu.HBM)
    bf16, f32 = jnp.bfloat16, jnp.float32
    results = pl.pallas_call(
        kernel,
        out_shape=(
            jax.ShapeDtypeStruct(stream_a.shape, bf16),
            jax.ShapeDtypeStruct(stream_b.shape, bf16),
            jax.ShapeDtypeStruct((16, 4), f32),
        ),
        in_specs=[hbm] * 6,
        out_specs=(vmem, vmem, vmem),
        scratch_shapes=[
            pltpu.VMEM((2, 8, features), bf16),
            pltpu.VMEM((TICKS, 2, 1, 2, 8), jnp.int32),
            pltpu.VMEM((2, 1, 4, features), bf16),
            pltpu.VMEM((2, quarter, QUARTERS * 256), bf16),
            pltpu.VMEM((2, 256, features), bf16),
            pltpu.VMEM((TICKS, 2, 64, quarter), bf16),
            pltpu.VMEM((TICKS, 2, 256, quarter), bf16),
            pltpu.VMEM((2, 128, quarter), f32),
            pltpu.VMEM((TICKS, 2, 128, quarter), bf16),
            pltpu.VMEM((TICKS, 2, 128, quarter), bf16),
            pltpu.VMEM((TICKS, 2, 128, quarter), bf16),
            pltpu.VMEM((TICKS, 2, 128, quarter), bf16),
            pltpu.VMEM((2, 32, quarter), bf16),
            pltpu.VMEM((2, 32, quarter), bf16),
            pltpu.VMEM((TICKS, 2, 8, 128), f32),
            pltpu.VMEM((2, 8, 128), f32),
            pltpu.VMEM((2, 16, quarter), bf16),
            pltpu.VMEM((2, 16, quarter), bf16),
            pltpu.VMEM((5, 16, 128), f32),
            pltpu.VMEM((5, SIDE - 1, 16, 128), f32),
            pltpu.SemaphoreType.DMA((TICKS, 2, KINDS)),
            pltpu.SemaphoreType.DMA((TICKS, 2, KINDS)),
            pltpu.SemaphoreType.DMA((4,)),
            pltpu.SemaphoreType.DMA((2, 2)),
            pltpu.SemaphoreType.DMA((2, 2)),
            pltpu.SemaphoreType.DMA((2, 2)),
            pltpu.SemaphoreType.DMA((2, 2)),
            pltpu.SemaphoreType.DMA((2, 2)),
            pltpu.SemaphoreType.DMA((5,)),
            pltpu.SemaphoreType.DMA((5,)),
        ],
        compiler_params=pltpu.CompilerParams(
            collective_id=0, has_side_effects=True, vmem_limit_bytes=55 * 2**20
        ),
        name="relay",
    )(
        stream_a, stream_b, jnp.swapaxes(routes, 3, 4), jnp.swapaxes(router_weight, 2, 3),
        up_weight, down_weight,
    )
    final_a, final_b, load = pl.pallas_call(
        hand_over,
        out_shape=(
            jax.ShapeDtypeStruct(stream_a.shape, bf16),
            jax.ShapeDtypeStruct(stream_b.shape, bf16),
            jax.ShapeDtypeStruct((4, 16), f32),
        ),
        in_specs=[vmem] * 3,
        out_specs=(vmem,) * 3,
        compiler_params=pltpu.CompilerParams(vmem_limit_bytes=55 * 2**20),
        name="hand_over",
    )(*results)
    return final_a, final_b, load.T


def solution(mesh):
    return jax.shard_map(
        shards,
        mesh=mesh,
        in_specs=(
            P("pipe", "expert", None),
            P("pipe", "expert", None),
            P(None, None, "pipe", "expert", None),
            P(None, "pipe", None, "expert"),
            P(None, "pipe", "expert", None),
            P(None, "pipe", None, None),
        ),
        out_specs=(P("pipe", "expert", None), P("pipe", "expert", None), P()),
        check_vma=False,
    )
```

```python
import jax
import jax.numpy as jnp
from jax import lax
from jax.experimental import pallas as pl
from jax.experimental.pallas import tpu as pltpu
from jax.sharding import PartitionSpec as P

TICKS = 2
EPS = 1e-06
QUARTERS = 4
CAP = 4
SIDE = 8
SECTIONS = 16
BLOCK = 16
MESH = pl.DeviceIdType.MESH

TO_OWN, TO_OTHER, ON_OWN, ON_OTHER, SWAP_OWN, SWAP_OTHER, HOME, RELAY = range(8)
TO_OTHER_FAR = 8
KINDS = 9


def kernel(
    sa, sb, routes_in, router_in, up, down,
    out_a, out_b, out_load,
    xin, routes, router, u, w, tx, rx, mine, swap_tx, swap_rx, home_tx, home_rx, xtx, xr,
    picks, picks_next, centroids, centroids_next, mtx, mrx,
    send, recv, inputs, wlocal, wsend, wrecv, psend, precv, msend, mrecv,
):
    quarter = u.shape[1]
    features = QUARTERS * quarter
    f32, bf16 = jnp.float32, jnp.bfloat16
    pipe = lax.axis_index("pipe")
    ex = lax.axis_index("expert")
    zh = ex // 16
    y = (ex // 2) % SIDE
    core = ex % 2
    turn = 1 - 2 * (y % 2)
    sibling = {"expert": ex + 1 - 2 * core}
    mate = {"expert": ex + 2 * turn}
    ahead = (pipe + 1) % SECTIONS
    behind = (pipe + SECTIONS - 1) % SECTIONS

    def at(plane, to):
        return plane * 16 + to * 2 + core

    targets = [(y + turn * step + SIDE) % SIDE for step in (0, -1, 2, -3)]
    sources = [(y - turn * k + SIDE) % SIDE for k in range(4)]

    px, pz = pipe % 4, pipe // 4
    x_mates = [{"pipe": pz * 4 + (px + k) % 4} for k in range(1, 4)]
    z_mates = [{"pipe": ((pz + k) % 4) * 4 + px} for k in range(1, 4)]

    def weight_parts(s, which):
        if which == 0:
            return [
                (
                    up.at[s, 0, pl.ds(q * quarter, quarter), :],
                    u.at[s, :, pl.ds(pl.multiple_of(q * 256 + core * 128, 128), 128)],
                )
                for q in range(QUARTERS)
            ]
        return [(down.at[s, 0], w.at[s, pl.ds(pl.multiple_of(core * 128, 128), 128), :])]

    barrier = pltpu.get_barrier_semaphore()

    def greet(device):
        pl.semaphore_signal(barrier, inc=1, device_id=device, device_id_type=MESH)

    near = [(y + step + SIDE) % SIDE for step in (2, -2)] + [
        (y + turn * step + SIDE) % SIDE for step in (-1, -3)
    ]
    greeted = [{"expert": at(1 - zh, to)} for to in near + [y]]
    greeted += [{"expert": at(zh, to)} for to in near] + [{"pipe": ahead}, {"pipe": behind}]
    greeted += x_mates + z_mates + [mate, sibling]
    for device in greeted:
        greet(device)

    input_copies = [
        pltpu.make_async_copy(src, dst, inputs.at[i])
        for i, (src, dst) in enumerate(
            (
                (sa.at[0], xin.at[0]),
                (sb.at[0], xin.at[1]),
                (routes_in, routes),
                (router_in, router),
            )
        )
    ]
    for copy in input_copies:
        copy.start()
    for s in range(2):
        for which in range(2):
            for src, dst in weight_parts(s, which):
                pltpu.make_async_copy(src, dst, wlocal.at[s, which]).start()

    def remote(src, dst, t, s, kind, device):
        return pltpu.make_async_remote_copy(
            src_ref=src, dst_ref=dst, send_sem=send.at[t, s, kind],
            recv_sem=recv.at[t, s, kind], device_id=device, device_id_type=MESH,
        )

    def drain(ref, sem):
        pltpu.make_async_copy(ref, ref, sem).wait()

    def half_of_weight(s, which):
        return u.at[s, :, pl.ds(0, 512)] if which == 0 else w.at[s, pl.ds(0, 128), :]

    def send_weights(s, which):
        for src, dst in weight_parts(s, which):
            pltpu.make_async_remote_copy(
                src_ref=src, dst_ref=dst, send_sem=wsend.at[s, which],
                recv_sem=wrecv.at[s, which], device_id=sibling, device_id_type=MESH,
            ).start()

    def iota(shape, dim):
        return lax.broadcasted_iota(jnp.int32, shape, dim)

    def across(a, b):
        return lax.dot_general(a, b, (((1,), (1,)), ((), ())), preferred_element_type=f32)

    lane4 = iota((8, 4), 1).astype(f32)
    low8 = (iota((8, 8), 0) > iota((8, 8), 1)).astype(bf16)
    eye8 = (iota((8, 8), 0) == iota((8, 8), 1)).astype(bf16)
    expert_hot = (iota((64, 4), 0) // BLOCK == iota((64, 4), 1)).astype(bf16)
    row_t, col_t = iota((64, 32), 0), iota((64, 32), 1)
    same_quarter = (row_t // 4) % 4 == col_t // 8
    slot_t = (row_t % 4).astype(f32)

    for copy in input_copies:
        copy.wait()

    for s in range(2):
        for t in range(TICKS):
            picks[t, s, :, 0:2] = across(eye8, routes[t, s, 0].astype(f32).astype(bf16))
        centroids[s] = jnp.concatenate(
            [
                router[s, 0, :, q * quarter : (q + 1) * quarter].astype(f32)
                for q in range(QUARTERS)
            ],
            axis=0,
        ).astype(bf16)

    def send_ahead_of_relay():
        for s, section in ((0, behind), (1, ahead)):
            for i, (src, dst) in enumerate(
                ((picks.at[1, s], picks_next.at[s]), (centroids.at[s], centroids_next.at[s]))
            ):
                pltpu.make_async_remote_copy(
                    src_ref=src, dst_ref=dst, send_sem=psend.at[s, i], recv_sem=precv.at[s, i],
                    device_id={"pipe": section}, device_id_type=MESH,
                ).start()

    def first_rows(s):
        return [
            xin[s, :, q * quarter : (q + 1) * quarter].astype(f32) for q in range(QUARTERS)
        ]

    def relayed_rows(ref, s):
        rows = ref[s].astype(f32)
        return [rows[q * 8 : (q + 1) * 8] for q in range(QUARTERS)]

    def seats(picked):
        member = [(picked[:, j : j + 1] == lane4).astype(f32) for j in range(2)]
        selected = member[0] + member[1]
        before = jnp.dot(low8, selected.astype(bf16), preferred_element_type=f32)
        slot = jnp.where(selected > 0, before, -1.0)
        return member, slot

    def placing(slot):
        slot_of = across(expert_hot, jnp.concatenate([slot] * QUARTERS, axis=0).astype(bf16))
        return jnp.where(same_quarter & (slot_of == slot_t), 1.0, 0.0).astype(bf16)

    def normalize(x):
        total = sum(jnp.sum(part * part, axis=1, keepdims=True) for part in x)
        scale = lax.rsqrt(total / features + EPS)
        return jnp.concatenate([part * scale for part in x], axis=0).astype(bf16)

    def gating(normed4, member, central):
        mixed = across(normed4, central)
        logits = sum(
            mixed[q * 8 : (q + 1) * 8, q * 4 : (q + 1) * 4] for q in range(QUARTERS)
        )
        affinity = jax.nn.sigmoid(logits)
        chosen = [jnp.sum(m * affinity, axis=1, keepdims=True) for m in member]
        both = chosen[0] + chosen[1]
        return (chosen[0] / both) * member[0] + (chosen[1] / both) * member[1]

    def pack(t, s, normed4, place):
        tx[t, s] = jnp.dot(place, normed4, preferred_element_type=f32).astype(bf16)

    def block(index):
        if isinstance(index, int):
            return pl.ds(index * BLOCK, BLOCK)
        return pl.ds(pl.multiple_of(index * BLOCK, BLOCK), BLOCK)

    def blocks(first, count):
        return pl.ds(first * BLOCK, count * BLOCK)

    def dispatch(t, s):
        for plane, kind, base in ((zh, TO_OWN, 0), (1 - zh, TO_OTHER, 4)):
            for k, to in reversed(list(enumerate(targets))):
                src = block(plane * 2 + to // 4)
                if base == 0 and k == 0:
                    over = {"expert": ex + 2 * turn}
                    if t > 0:
                        over["pipe"] = ahead if s == 0 else behind
                    remote(
                        tx.at[t, s, src], rx.at[t, s, block(8)], t, s, ON_OWN, over
                    ).start()
                if t == 0 and base == 0 and k == 0:
                    rx[t, s, block(0)] = tx[t, s, src]
                    continue
                device = {"expert": at(plane, to)}
                if t > 0:
                    device["pipe"] = ahead if s == 0 else behind
                by = TO_OTHER_FAR if base == 4 and k > 1 else kind
                remote(
                    tx.at[t, s, src], rx.at[t, s, block(base + k)], t, s, by, device
                ).start()

    def pass_on(t, s, group):
        if group == 1:
            for kind, first in ((TO_OTHER_FAR, 6), (TO_OTHER, 4)):
                drain(rx.at[t, s, blocks(first, 2)], recv.at[t, s, kind])
                remote(
                    rx.at[t, s, blocks(first, 2)], rx.at[t, s, blocks(8 + first, 2)],
                    t, s, ON_OTHER, mate,
                ).start()
            return
        got = blocks(1, 3) if t == 0 else blocks(0, 4)
        drain(rx.at[t, s, got], recv.at[t, s, TO_OWN + group])
        remote(
            rx.at[t, s, blocks(1, 3)], rx.at[t, s, blocks(9, 3)], t, s, ON_OWN, mate
        ).start()

    def experts(t, s):
        drain(rx.at[t, s, blocks(8, 4)], recv.at[t, s, ON_OWN])
        drain(rx.at[t, s, blocks(12, 4)], recv.at[t, s, ON_OTHER])
        if t == 0:
            drain(half_of_weight(s, 0), wlocal.at[s, 0])
            drain(half_of_weight(s, 0), wrecv.at[s, 0])
        arrived = rx[t, s]
        lower = iota((16, 8, 256), 1) < 4
        lifted = [
            jnp.dot(
                arrived, u[s, :, q * 256 : (q + 1) * 256], preferred_element_type=f32
            ).reshape(16, 2, 8, 256)
            for q in range(QUARTERS)
        ]
        part = jnp.where(lower, lifted[0][:, 0], lifted[1][:, 0]) + jnp.where(
            lower, lifted[2][:, 1], lifted[3][:, 1]
        )
        part = part.reshape(128, 256)
        lower2 = iota((128, 256), 0) % 8 < 4
        other = jnp.where(lower2, pltpu.roll(part, 124, 0), pltpu.roll(part, 4, 0))
        hidden = jax.nn.silu(part + other).astype(bf16)
        if t == 0:
            drain(half_of_weight(s, 1), wlocal.at[s, 1])
            drain(half_of_weight(s, 1), wrecv.at[s, 1])
        lower3 = iota((128, quarter), 0) % 8 < 4
        halves = []
        for h in range(2):
            two = [
                jnp.dot(
                    hidden, w[s, :, q * quarter : (q + 1) * quarter], preferred_element_type=f32
                )
                for q in (2 * h, 2 * h + 1)
            ]
            halves.append(jnp.where(lower3, two[0], two[1]).reshape(16, 1, 8, quarter))
        both = jnp.concatenate(halves, axis=1).reshape(256, quarter)
        mine[s] = both[0:128]
        swap_tx[t, s] = both[128:256].astype(bf16)
        swap(t, s, 1)

    def swap(t, s, group):
        rows = blocks(group * 4, 4)
        remote(
            swap_tx.at[t, s, rows], swap_rx.at[t, s, rows], t, s, SWAP_OWN + group, mate
        ).start()

    def send_home(t, s, group):
        slot = zh * 4 + y // 2
        plane = 1 - zh if group else zh
        rows = blocks(group * 4, 4)
        drain(swap_rx.at[t, s, rows], recv.at[t, s, SWAP_OWN + group])
        home_tx[t, s, rows] = (mine[s, rows] + swap_rx[t, s, rows].astype(f32)).astype(bf16)
        for k, to in reversed(list(enumerate(sources))):
            if group == 0 and k == 0:
                home_rx[t, s, block(slot)] = home_tx[t, s, block(0)]
                continue
            remote(
                home_tx.at[t, s, block(group * 4 + k)], home_rx.at[t, s, block(slot)],
                t, s, HOME, {"expert": at(plane, to)},
            ).start()

    def finish(t, s, x, gates, slot):
        drain(home_rx.at[t, s, blocks(0, 7)], recv.at[t, s, HOME])
        terms = []
        for e in range(4):
            two = home_rx[t, s, blocks(2 * e, 2)].astype(f32)
            sums = two[0:BLOCK] + two[BLOCK : 2 * BLOCK]
            for c in range(CAP):
                factor = jnp.where(slot[:, e : e + 1] == c, gates[:, e : e + 1], 0.0)
                terms.append((sums, c, factor))
        rows = []
        for q in range(QUARTERS):
            total = x[q]
            for sums, c, factor in terms:
                total = total + factor * sums[q * 4 + c : q * 4 + c + 1, :]
            rows.append(total)
        return rows

    spread = [{"expert": at(zh, to)} for to in targets[1:]]
    spread += [{"expert": at(1 - zh, to)} for to in targets]
    rounds = [[sibling], spread, [mate], x_mates, z_mates]

    def mass_send(k):
        for i, device in enumerate(rounds[k]):
            pltpu.make_async_remote_copy(
                src_ref=mtx.at[k], dst_ref=mrx.at[k, i], send_sem=msend.at[k],
                recv_sem=mrecv.at[k], device_id=device, device_id_type=MESH,
            ).start()

    def mass_take(k):
        count = len(rounds[k])
        drain(mrx.at[k, pl.ds(0, count)], mrecv.at[k])
        return sum((mrx[k, i] for i in range(count)), mtx[k])

    def mass_step(k):
        mtx[k + 1] = mass_take(k)
        mass_send(k + 1)

    x = [first_rows(s) for s in range(2)]
    routed = [None, None]
    seated = [[seats(picks[t, s]) for s in range(2)] for t in range(TICKS)]
    for s in range(2):
        normed4 = normalize(x[s])
        member, slot = seated[0][s]
        pack(0, s, normed4, placing(slot))
        routed[s] = (gating(normed4, member, centroids[s]), slot)
    pl.semaphore_wait(barrier, len(greeted))
    row = iota((16, 4), 0)

    def mass_rows(gates, layer):
        return jnp.where(row == layer, jnp.sum(gates, axis=0, keepdims=True), 0.0)

    masses = [mass_rows(routed[0][0], pipe) + mass_rows(routed[1][0], SECTIONS - 1 - pipe)]

    def first(s):
        dispatch(0, s)
        if s == 1:
            send_ahead_of_relay()

    next_seats = [None, None]

    def look_ahead(s):
        drain(picks_next.at[s], precv.at[s, 0])
        drain(centroids_next.at[s], precv.at[s, 1])
        member, slot = seats(picks_next[s])
        next_seats[s] = (member, placing(slot))

    def between(s):
        xtx[s] = jnp.concatenate(finish(0, s, x[s], *routed[s]), axis=0).astype(bf16)
        normed4 = normalize(relayed_rows(xtx, s))
        member, place = next_seats[s]
        pack(1, s, normed4, place)
        dispatch(1, s)
        remote(
            xtx.at[s], xr.at[s], 0, s, RELAY, {"pipe": ahead if s == 0 else behind}
        ).start()
        gates = gating(normed4, member, centroids_next[s])
        masses.append(mass_rows(gates, ahead if s == 0 else SECTIONS - 1 - behind))

    def mass_start():
        mtx[0] = jnp.zeros_like(mtx[0])
        mtx[0, :, 0:4] = sum(masses)
        mass_send(0)

    def again(s):
        drain(xr.at[s], recv.at[0, s, RELAY])
        x[s] = relayed_rows(xr, s)
        member, slot = seated[1][s]
        routed[s] = (gating(normalize(x[s]), member, centroids[s]), slot)

    def last(s):
        rows = finish(1, s, x[s], *routed[s])
        ref = out_a if s == 0 else out_b
        for q in range(QUARTERS):
            ref[0, :, q * quarter : (q + 1) * quarter] = rows[q].astype(bf16)

    first(0)
    first(1)
    send_weights(0, 0)
    send_weights(0, 1)
    send_weights(1, 0)
    send_weights(1, 1)
    pass_on(0, 0, 0)
    pass_on(0, 1, 0)
    pass_on(0, 0, 1)
    pass_on(0, 1, 1)
    experts(0, 0)
    experts(0, 1)
    swap(0, 0, 0)
    swap(0, 1, 0)
    look_ahead(0)
    look_ahead(1)
    send_home(0, 0, 1)
    send_home(0, 1, 1)
    send_home(0, 0, 0)
    send_home(0, 1, 0)
    between(0)
    between(1)
    mass_start()
    pass_on(1, 0, 0)
    mass_step(0)
    pass_on(1, 1, 0)
    pass_on(1, 0, 1)
    pass_on(1, 1, 1)
    again(0)
    again(1)
    experts(1, 0)
    mass_step(1)
    experts(1, 1)
    swap(1, 0, 0)
    swap(1, 1, 0)
    mass_step(2)
    send_home(1, 0, 1)
    send_home(1, 1, 1)
    send_home(1, 0, 0)
    send_home(1, 1, 0)
    mass_step(3)
    last(0)
    last(1)
    out_load[...] = mass_take(4)[:, 0:4] / (2 * TICKS * 8 * 32)

    for s in range(2):
        for which in range(2):
            drain(half_of_weight(s, which), wsend.at[s, which])
        drain(picks_next.at[s], psend.at[s, 0])
        drain(centroids_next.at[s], psend.at[s, 1])
    for k in range(5):
        drain(mrx.at[k, pl.ds(0, len(rounds[k]))], msend.at[k])
    for s in range(2):
        drain(xr.at[s], send.at[0, s, RELAY])
        for t in range(TICKS):
            drain(rx.at[t, s, blocks(0, 3 + t)], send.at[t, s, TO_OWN])
            for kind in (TO_OTHER, TO_OTHER_FAR):
                drain(rx.at[t, s, blocks(0, 2)], send.at[t, s, kind])
            for kind in (ON_OWN, ON_OTHER, SWAP_OWN, SWAP_OTHER):
                drain(rx.at[t, s, blocks(0, 4)], send.at[t, s, kind])
            drain(home_rx.at[t, s, blocks(0, 7)], send.at[t, s, HOME])


def hand_over(a, b, load, out_a, out_b, out_load):
    out_a[...] = a[...]
    out_b[...] = b[...]
    out_load[...] = load[...].T


def shards(stream_a, stream_b, routes, up_weight, down_weight, router_weight):
    features = stream_a.shape[2]
    quarter = features // QUARTERS
    vmem = pl.BlockSpec(memory_space=pltpu.VMEM)
    hbm = pl.BlockSpec(memory_space=pltpu.HBM)
    bf16, f32 = jnp.bfloat16, jnp.float32
    results = pl.pallas_call(
        kernel,
        out_shape=(
            jax.ShapeDtypeStruct(stream_a.shape, bf16),
            jax.ShapeDtypeStruct(stream_b.shape, bf16),
            jax.ShapeDtypeStruct((16, 4), f32),
        ),
        in_specs=[hbm] * 6,
        out_specs=(vmem, vmem, vmem),
        scratch_shapes=[
            pltpu.VMEM((2, 8, features), bf16),
            pltpu.VMEM((TICKS, 2, 1, 2, 8), jnp.int32),
            pltpu.VMEM((2, 1, 4, features), bf16),
            pltpu.VMEM((2, quarter, QUARTERS * 256), bf16),
            pltpu.VMEM((2, 256, features), bf16),
            pltpu.VMEM((TICKS, 2, 64, quarter), bf16),
            pltpu.VMEM((TICKS, 2, 256, quarter), bf16),
            pltpu.VMEM((2, 128, quarter), f32),
            pltpu.VMEM((TICKS, 2, 128, quarter), bf16),
            pltpu.VMEM((TICKS, 2, 128, quarter), bf16),
            pltpu.VMEM((TICKS, 2, 128, quarter), bf16),
            pltpu.VMEM((TICKS, 2, 128, quarter), bf16),
            pltpu.VMEM((2, 32, quarter), bf16),
            pltpu.VMEM((2, 32, quarter), bf16),
            pltpu.VMEM((TICKS, 2, 8, 128), f32),
            pltpu.VMEM((2, 8, 128), f32),
            pltpu.VMEM((2, 16, quarter), bf16),
            pltpu.VMEM((2, 16, quarter), bf16),
            pltpu.VMEM((5, 16, 128), f32),
            pltpu.VMEM((5, SIDE - 1, 16, 128), f32),
            pltpu.SemaphoreType.DMA((TICKS, 2, KINDS)),
            pltpu.SemaphoreType.DMA((TICKS, 2, KINDS)),
            pltpu.SemaphoreType.DMA((4,)),
            pltpu.SemaphoreType.DMA((2, 2)),
            pltpu.SemaphoreType.DMA((2, 2)),
            pltpu.SemaphoreType.DMA((2, 2)),
            pltpu.SemaphoreType.DMA((2, 2)),
            pltpu.SemaphoreType.DMA((2, 2)),
            pltpu.SemaphoreType.DMA((5,)),
            pltpu.SemaphoreType.DMA((5,)),
        ],
        compiler_params=pltpu.CompilerParams(
            collective_id=0, has_side_effects=True, vmem_limit_bytes=55 * 2**20
        ),
        name="relay",
    )(
        stream_a, stream_b, jnp.swapaxes(routes, 3, 4), jnp.swapaxes(router_weight, 2, 3),
        up_weight, down_weight,
    )
    final_a, final_b, load = pl.pallas_call(
        hand_over,
        out_shape=(
            jax.ShapeDtypeStruct(stream_a.shape, bf16),
            jax.ShapeDtypeStruct(stream_b.shape, bf16),
            jax.ShapeDtypeStruct((4, 16), f32),
        ),
        in_specs=[vmem] * 3,
        out_specs=(vmem,) * 3,
        compiler_params=pltpu.CompilerParams(vmem_limit_bytes=55 * 2**20),
        name="hand_over",
    )(*results)
    return final_a, final_b, load.T


def solution(mesh):
    return jax.shard_map(
        shards,
        mesh=mesh,
        in_specs=(
            P("pipe", "expert", None),
            P("pipe", "expert", None),
            P(None, None, "pipe", "expert", None),
            P(None, "pipe", None, "expert"),
            P(None, "pipe", "expert", None),
            P(None, "pipe", None, None),
        ),
        out_specs=(P("pipe", "expert", None), P("pipe", "expert", None), P()),
        check_vma=False,
    )
```
